32 devices in a mesh: groups: 1, row: 16 (over z, y, core), col: 2 (over x), freq: 1.
Axes of the slice: x: 2, y: 2, z: 4, core: 2. Of those that a mesh axis runs over, the one named last changes fastest.
Arguments:
- traces: bfloat16 [256, 96000], P(('groups', 'row', 'col')), may hold values from -6 to 6
- slot_channel: int32 [256], P(('groups', 'row', 'col')), may hold values from 0 to 255, as said below
- usable_blocks: int32 [32], P(('groups', 'row', 'col')), may hold values 0 or 1
Outputs:
- correlation: float32 [65, 256, 256], P(None, ('groups', 'row'), ('col', 'freq'))
The draws below stay inside these ranges and needn't reach their ends.
Inputs may be any that keep to these rules, and one draw needn't show every extreme that they name: `slot_channel`: every channel is recorded in exactly one slot, and the 16 slots of each aligned block of 16 slots hold the 16 fiber channels of that same block.
All inputs are finite; a program needn't handle non-finite values. No bound on the sum of `usable_blocks` on one device may be relied on, other than what follows from the above.
Results may differ from the reference program's by a relative error of at most 0.0054.
Values may be sent and summed in bfloat16 or wider, within the bound.
A program may use at most 64 MiB of HBM per device.

```python
import math
import jax
import jax.numpy as jnp
from jax import lax

CH_DEV = 8
SEG = 300
FREQS = 64
MAXLAG = 32
LAGS = 65
SEGS = 320
RB = 16
C = 256
NFLAG = 32
N_ROW = 16
N_COL = 2


def draw_slot_channel(key, part):
    key = jax.random.fold_in(key, 11)
    block_keys = jax.random.split(key, C // RB)

    def block_order(block_key):
        return jax.random.permutation(block_key, RB).astype(jnp.int32)
    orders = jax.vmap(block_order)(block_keys)
    offsets = (jnp.arange(C // RB, dtype=jnp.int32) * RB)[:, None]
    return (orders + offsets).reshape(C)


def with_ends(array, key, smallest, largest):
    extent = array.shape
    place = [jax.random.randint(jax.random.fold_in(key, axis), (), 0, extent[axis]) for axis in range(len(extent))]
    array = array.at[tuple(place)].set(smallest)
    longest = extent.index(max(extent))
    place[longest] = (place[longest] + 1) % extent[longest]
    return array.at[tuple(place)].set(largest)


def steps_of(key, shape, shards, low, top_value):
    loudness, own = 1.0, jax.random.fold_in(key, 6)
    for position, parts in shards:
        heights = jnp.exp(jax.random.uniform(jax.random.fold_in(own, position), (parts,), jnp.float32, low / len(shards), top_value / len(shards)))
        loudness = loudness * jnp.repeat(heights, shape[position] // parts).reshape([-1 if axis == position else 1 for axis in range(len(shape))])
    return loudness


def centred(stream_key, shape, spread, limit, cuts=(), kind=jnp.bfloat16):
    loudness = steps_of(stream_key, shape, cuts, -0.22, 0.18) if cuts else 1.0
    entries = jax.random.normal(stream_key, shape, jnp.float32) * spread * loudness
    return jnp.minimum(jnp.maximum(entries, -limit), limit).astype(kind)


def setup_inputs(seed: int = 0, part: int = 0) -> dict:
    key_of = jax.random.split(jax.random.key(seed), 4)
    part_keys = jax.random.split(jax.random.fold_in(key_of[3], part), 4)
    traces = centred(part_keys[0], (C, SEGS * SEG), 1.0, 6.0, ((0, 32),))
    slot_channel = draw_slot_channel(jax.random.fold_in(jax.random.fold_in(key_of[3], part), 71), part)
    usable_blocks = with_ends((jax.random.randint(part_keys[2], (NFLAG,), 0, 4) < 3).astype(jnp.int32), jax.random.fold_in(part_keys[2], 1), 0, 1)
    return {"traces": traces, "slot_channel": slot_channel, "usable_blocks": usable_blocks}


water_level = 0.5
corr_gain = 3.0

def taper_window():
    samples = jnp.arange(SEG, dtype=jnp.int32)
    taper = 0.5 - 0.5 * jnp.cos(2.0 * math.pi / SEG * samples.astype(jnp.float32))
    return (samples, taper)

def reference(traces, slot_channel, usable_blocks):
    ordered = jnp.zeros_like(traces).at[slot_channel].set(traces)
    samples, taper = taper_window()
    bin_numbers = 1 + jnp.arange(FREQS, dtype=jnp.int32)
    turns = samples[:, None] * bin_numbers[None, :] % SEG
    angles = 2.0 * math.pi / SEG * turns.astype(jnp.float32)
    dft_table = jnp.concatenate([taper[:, None] * jnp.cos(angles), -taper[:, None] * jnp.sin(angles)], axis=1).astype(jnp.bfloat16)
    pieces = ordered.reshape(C, SEGS, SEG)
    coefficients = jnp.einsum('csn,nq->csq', pieces.astype(jnp.float32), dft_table.astype(jnp.float32))
    windowed = pieces.astype(jnp.float32) * taper
    level = jnp.sqrt(SEG * (lax.optimization_barrier(jnp.mean(windowed * windowed, axis=-1)) + 1e-05))
    real_part = coefficients[..., :FREQS]
    imag_part = coefficients[..., FREQS:]
    divisor = jnp.sqrt(real_part * real_part + imag_part * imag_part) + water_level * level[..., None]
    usable = jnp.repeat(usable_blocks, CH_DEV).astype(jnp.bfloat16)[:, None, None]
    white_real = (real_part / divisor).astype(jnp.bfloat16) * usable
    white_imag = (imag_part / divisor).astype(jnp.bfloat16) * usable
    spectra = jnp.concatenate([jnp.transpose(white_real, (0, 2, 1)), jnp.transpose(white_imag, (0, 2, 1))], axis=-1)
    spectra_wide = spectra.astype(jnp.float32)
    lag_steps = jnp.arange(LAGS, dtype=jnp.int32) - MAXLAG
    lag_turns = lag_steps[:, None] * bin_numbers[None, :] % SEG
    lag_angles = 2.0 * math.pi / SEG * lag_turns.astype(jnp.float32)
    norm_gain = corr_gain / math.sqrt(SEGS * FREQS)
    lag_table = jnp.stack([norm_gain * jnp.cos(lag_angles), -norm_gain * jnp.sin(lag_angles)], axis=-1).astype(jnp.bfloat16).astype(jnp.float32)

    def block_rows(index):
        row_side = lax.dynamic_slice_in_dim(spectra, (index * RB).astype(jnp.int32), RB, 0)
        rotated = jnp.concatenate([row_side[..., SEGS:], -row_side[..., :SEGS]], axis=-1)
        stacked_rows = jnp.concatenate([row_side, rotated], axis=0).astype(jnp.float32)
        cross = jnp.einsum('afk,bfk->fab', stacked_rows, spectra_wide)
        stacked = cross.astype(jnp.bfloat16).astype(jnp.float32).reshape(FREQS, 2, RB, C)
        lagged = jnp.einsum('lfp,fpab->lab', lag_table, stacked)
        row_ids = index * RB + jnp.arange(RB, dtype=jnp.int32)
        same = row_ids[:, None] == jnp.arange(C, dtype=jnp.int32)[None, :]
        lagged = jnp.where(same[None, :, :], jnp.float32(0.0), lagged)
        lagged = lagged.reshape(LAGS, RB, N_ROW, N_COL, CH_DEV)
        return jnp.transpose(lagged, (0, 1, 3, 2, 4)).reshape(LAGS, RB, C)
    blocks = lax.map(block_rows, jnp.arange(N_ROW, dtype=jnp.int32))
    return jnp.transpose(blocks, (1, 0, 2, 3)).reshape(LAGS, C, C)
```

```python
import functools
import math

import jax
import jax.numpy as jnp
import numpy as np
from jax import lax
from jax.experimental import pallas as pl
from jax.experimental.pallas import tpu as pltpu
from jax.sharding import PartitionSpec as P

SEG = 300
FREQS = 64
MAXLAG = 32


water_level = 0.5
corr_gain = 3.0


def lag_weights(bin_numbers, segment_total):
    lag_steps = jnp.arange(2 * MAXLAG + 1, dtype=jnp.int32) - MAXLAG
    lag_turns = lag_steps[:, None] * bin_numbers[None, :] % SEG
    lag_angles = 2.0 * math.pi / SEG * lag_turns.astype(jnp.float32)
    norm_gain = corr_gain / math.sqrt(segment_total * FREQS)
    return jnp.stack(
        [norm_gain * jnp.cos(lag_angles), -norm_gain * jnp.sin(lag_angles)], axis=-1
    ).astype(jnp.bfloat16)

def gather_body(traces, slot_channel, usable_blocks):
    own_count = traces.shape[0]
    segment_total = traces.shape[1] // SEG
    local_bins = FREQS // lax.axis_size("freq")
    freq_index = lax.axis_index("freq")
    row_index = lax.axis_index("row")
    col_index = lax.axis_index("col")
    samples = jnp.arange(SEG, dtype=jnp.int32)
    taper = 0.5 - 0.5 * jnp.cos(2.0 * math.pi / SEG * samples.astype(jnp.float32))
    bin_numbers = 1 + freq_index * local_bins + jnp.arange(local_bins, dtype=jnp.int32)
    turns = samples[:, None] * bin_numbers[None, :] % SEG
    angles = 2.0 * math.pi / SEG * turns.astype(jnp.float32)
    dft_table = jnp.concatenate(
        [taper[:, None] * jnp.cos(angles), -taper[:, None] * jnp.sin(angles)], axis=1
    ).astype(jnp.bfloat16)
    pieces = traces.reshape(own_count, segment_total, SEG)
    coefficients = jnp.einsum("csn,nq->csq", pieces, dft_table, preferred_element_type=jnp.float32)
    windowed = pieces.astype(jnp.float32) * taper
    level = jnp.sqrt(SEG * (jnp.mean(windowed * windowed, axis=-1) + 1e-05))
    real_part = coefficients[..., :local_bins]
    imag_part = coefficients[..., local_bins:]
    divisor = (
        jnp.sqrt(real_part * real_part + imag_part * imag_part) + water_level * level[..., None]
    )
    white_real = jnp.transpose((real_part / divisor).astype(jnp.bfloat16), (0, 2, 1))
    white_imag = jnp.transpose((imag_part / divisor).astype(jnp.bfloat16), (0, 2, 1))
    own_spectra = jnp.concatenate([white_real, white_imag], axis=-1)
    block_spectra, block_slots, block_usable = (
        lax.all_gather(own_spectra, "col", axis=0, tiled=True),
        lax.all_gather(slot_channel, "col", axis=0, tiled=True),
        lax.all_gather(usable_blocks, "col", axis=0, tiled=True),
    )
    block_size = block_spectra.shape[0]
    positions = block_slots % block_size
    one_hot = (positions[None, :] == jnp.arange(block_size, dtype=jnp.int32)[:, None]).astype(
        jnp.bfloat16
    )
    ordered = jnp.einsum(
        "us,sfk->ufk", one_hot, block_spectra, preferred_element_type=jnp.float32
    ).astype(jnp.bfloat16)
    usable = jnp.repeat(block_usable, own_count, total_repeat_length=block_size).astype(
        jnp.bfloat16
    )
    ordered = ordered * usable[:, None, None]
    rotated = jnp.concatenate(
        [ordered[..., segment_total:], -ordered[..., :segment_total]], axis=-1
    )
    stacked_rows = jnp.concatenate([ordered, rotated], axis=0)
    quarter = lax.dynamic_slice_in_dim(ordered, col_index * own_count, own_count, 0)
    column_total = own_count * lax.axis_size("row")
    empty_sum = jnp.zeros((local_bins, 2 * block_size, column_total), jnp.float32)
    product = jnp.einsum(
        "afk,bfk->fab",
        stacked_rows,
        lax.all_gather(quarter, "row", axis=0, tiled=True),
        preferred_element_type=jnp.float32,
    )
    cross = lax.dynamic_update_slice_in_dim(empty_sum, product, jnp.int32(0), 2)
    stacked = cross.astype(jnp.bfloat16).reshape(local_bins, 2, block_size, column_total)
    lag_table = lag_weights(bin_numbers, segment_total)
    partial_lags = jnp.einsum(
        "lfp,fpab->lab", lag_table, stacked, preferred_element_type=jnp.float32
    )
    result = lax.psum_scatter(partial_lags, "freq", scatter_dimension=2, tiled=True)
    out_width = result.shape[2]
    columns = freq_index * out_width + jnp.arange(out_width, dtype=jnp.int32)
    column_block = columns // own_count
    column_place = col_index * own_count + columns % own_count
    row_place = jnp.arange(block_size, dtype=jnp.int32)
    same = (column_block[None, :] == row_index) & (row_place[:, None] == column_place[None, :])
    return jnp.where(same[None, :, :], jnp.float32(0.0), result)


LANES = 128
SPAN = SEG * LANES // math.gcd(SEG, LANES)
SPAN_SEGS = SPAN // SEG
WIDE = -(-SEG // LANES) * LANES
HALF = LANES // 2
LAGS = 2 * MAXLAG + 1
LAG_ROWS = -(-LAGS // 16) * 16


def spectrum_table():
    taper = 0.5 - 0.5 * np.cos(2.0 * np.pi / SEG * np.arange(SEG))
    angles = 2.0 * np.pi / SEG * (np.arange(SEG)[:, None] * np.arange(1, FREQS + 1)[None, :] % SEG)
    table = np.zeros((WIDE, 2 * FREQS), np.float32)
    table[:SEG] = taper[:, None] * np.concatenate([np.cos(angles), -np.sin(angles)], axis=1)
    wide_taper = np.zeros((8, WIDE), np.float32)
    wide_taper[:, :SEG] = taper
    return table.astype(jnp.bfloat16), wide_taper


def lag_table(segment_total):
    turns = (np.arange(LAGS) - MAXLAG)[:, None] * np.arange(1, FREQS + 1)[None, :] % SEG
    angles = 2.0 * np.pi / SEG * turns
    gain = corr_gain / math.sqrt(segment_total * FREQS)
    table = np.zeros((LAG_ROWS, FREQS, 2), np.float32)
    table[:LAGS, :, 0] = gain * np.cos(angles)
    table[:LAGS, :, 1] = -gain * np.sin(angles)
    return table.reshape(LAG_ROWS, 2 * FREQS).astype(jnp.bfloat16)


def exchange_kernel(
    rows, cols, traces, slots, usable, table, taper, lags, out,
    samples, levels, white, spectra, send1, recv1, meta, recv_meta, send2, recv2, wide2, lagged,
    s1, r1, sm, rm, s2, r2, own,
):
    f32, bf16 = jnp.float32, jnp.bfloat16
    count = rows * cols
    bins = FREQS // count
    own_count = traces.shape[0]
    block = own_count * cols
    channels = own_count * count
    group = bins * own_count
    spans = traces.shape[1] // SPAN
    row_index, col_index = lax.axis_index("row"), lax.axis_index("col")
    me = row_index * cols + col_index

    def peer(step):
        other = lax.rem(me + step, count)
        return other, {"row": other // cols, "col": lax.rem(other, cols)}

    barrier = pltpu.get_barrier_semaphore()

    def greet(step, carry):
        pl.semaphore_signal(
            barrier, inc=1, device_id=peer(step)[1], device_id_type=pl.DeviceIdType.MESH
        )
        return carry

    lax.fori_loop(1, count, greet, 0)

    sub = lax.broadcasted_iota(jnp.int32, (group, LANES), 0)
    lane = lax.broadcasted_iota(jnp.int32, (group, LANES), 1)
    place = jnp.zeros((group, LANES), jnp.int32)
    for u in range(own_count):
        place = jnp.where(sub % own_count == u, slots[u], place)
    place = place + sub // own_count * channels
    meta[...] = jnp.where(lane < HALF, place, usable[0])

    def one_span(span, carry):
        for s in range(0, SPAN_SEGS, 2):
            pair = []
            for q in (s, s + 1):
                base = q * SEG // LANES * LANES
                shift = q * SEG - base
                width = -(-(shift + SEG) // LANES) * LANES
                x = traces[:, pl.ds(pl.multiple_of(span * SPAN + base, LANES), width)].astype(f32)
                if shift:
                    x = pltpu.roll(x, width - shift, 1)
                x = x[:, :WIDE]
                windowed = x * taper[...]
                power = jnp.sum(windowed * windowed, axis=1, keepdims=True)
                level = water_level * jnp.sqrt(power + SEG * 1e-05)
                levels[q * own_count : (q + 1) * own_count, :] = jnp.broadcast_to(
                    level, (own_count, LANES)
                )
                pair.append(x)
            samples[s * own_count : (s + 2) * own_count, :] = jnp.concatenate(pair, 0).astype(bf16)
        y = jnp.dot(samples[...], table[...], preferred_element_type=f32)
        square = y * y
        magnitude = jnp.sqrt(square + pltpu.roll(square, FREQS, 1))
        depth = SPAN_SEGS * own_count
        white[pl.ds(pl.multiple_of(span * depth, depth), depth), :] = y / (magnitude + levels[...])
        return carry

    lax.fori_loop(0, spans, one_span, 0)

    for u in range(own_count):
        strip = pl.ds(u, FREQS, stride=own_count)
        for t in range(2):
            z = white[pl.ds(t * LANES * own_count + u, LANES, stride=own_count), :].T
            spectra[t, strip, :] = z[:FREQS]
            spectra[3 + t, strip, :] = z[FREQS:]
        z = white[pl.ds(2 * LANES * own_count + u, HALF, stride=own_count), :]
        z = jnp.concatenate([z, pltpu.roll(z, FREQS, 1)], 0).T
        spectra[2, strip, :] = z[:FREQS]
    for t in range(5):
        send1[:, :, t * LANES : (t + 1) * LANES] = (
            spectra[t].astype(bf16).reshape(count, group, LANES)
        )

    pl.semaphore_wait(barrier, count - 1)

    def remote(src, dst, send_sem, recv_sem, target):
        return pltpu.make_async_remote_copy(
            src_ref=src, dst_ref=dst, send_sem=send_sem, recv_sem=recv_sem,
            device_id=target, device_id_type=pl.DeviceIdType.MESH,
        )

    def first(step):
        other, target = peer(step)
        return (
            remote(meta, recv_meta.at[me], sm.at[other], rm.at[me], target),
            remote(send1.at[other], recv1.at[me], s1.at[other], r1.at[me], target),
        )

    def second(step):
        other, target = peer(step)
        return remote(send2.at[other], recv2.at[me], s2.at[other], r2.at[me], target)

    def start_first(step, carry):
        for copy in first(step):
            copy.start()
        return carry

    lax.fori_loop(1, count, start_first, 0)
    kept = pltpu.make_async_copy(send1.at[me], recv1.at[me], own.at[0])
    kept.start()
    recv_meta[me] = meta[...]
    kept.wait()

    def wait_first(step, carry):
        other, target = peer(step)
        remote(meta, recv_meta.at[other], sm.at[other], rm.at[other], target).wait()
        remote(send1.at[other], recv1.at[other], s1.at[other], r1.at[other], target).wait()
        return carry

    lax.fori_loop(1, count, wait_first, 0)

    known = recv_meta[...]
    target_row = known.reshape(count * group, LANES).astype(f32).T[0:1, :]
    good = known[:, :own_count, HALF : HALF + 1].reshape(channels, 1).astype(f32)
    gathered = recv1[...].reshape(count * group, 5 * LANES)
    lane_sign = jnp.where(lax.broadcasted_iota(jnp.int32, (1, LANES), 1) < HALF, 1.0, -1.0)
    for b in range(bins):
        row_number = lax.broadcasted_iota(jnp.int32, (channels, 1), 0) + b * channels
        pick = jnp.where(row_number.astype(f32) == target_row, good, 0.0).astype(bf16)
        ordered = jnp.dot(pick, gathered, preferred_element_type=f32)
        mid = pltpu.roll(ordered[:, 2 * LANES : 3 * LANES], HALF, 1) * lane_sign
        rotated = jnp.concatenate(
            [ordered[:, 3 * LANES :], mid, -ordered[:, : 2 * LANES]], axis=1
        )
        by_column = jnp.swapaxes(ordered.reshape(rows, cols, own_count, 5 * LANES), 0, 1)
        by_column = by_column.reshape(channels, 5 * LANES).astype(bf16)
        for p, left in enumerate((ordered, rotated)):
            cross = lax.dot_general(
                left.astype(bf16), by_column, (((1,), (1,)), ((), ())), preferred_element_type=f32
            ).astype(bf16)
            width = channels // cols
            for r in range(rows):
                for c in range(cols):
                    send2[r * cols + c, (2 * b + p) * block : (2 * b + p + 1) * block, :] = cross[
                        r * block : (r + 1) * block, c * width : (c + 1) * width
                    ]

    def start_second(step, carry):
        second(step).start()
        return carry

    lax.fori_loop(1, count, start_second, 0)
    kept = pltpu.make_async_copy(send2.at[me], recv2.at[me], own.at[1])
    kept.start()
    kept.wait()

    def wait_second(step, carry):
        other, target = peer(step)
        remote(send2.at[other], recv2.at[other], s2.at[other], r2.at[other], target).wait()
        return carry

    lax.fori_loop(1, count, wait_second, 0)

    wide2[...] = recv2[...].astype(f32).reshape(wide2.shape)
    column = lax.broadcasted_iota(jnp.int32, (1, LANES), 1)
    for a in range(block):
        piece = wide2[pl.ds(a, 2 * FREQS, stride=block), :].astype(bf16)
        answer = jnp.dot(lags[...], piece, preferred_element_type=f32)[:LAGS]
        same = (column // own_count == row_index) & (
            col_index * own_count + column % own_count == a
        )
        lagged[pl.ds(a, LAGS, stride=block), :] = jnp.where(same, 0.0, answer)
    out[...] = lagged[...].reshape(out.shape)


def exchange_body(rows, cols, traces, slot_channel, usable_blocks):
    own_count = traces.shape[0]
    segment_total = traces.shape[1] // SEG
    count = rows * cols
    bins = FREQS // count
    block = own_count * cols
    channels = own_count * count
    group = bins * own_count
    table, taper = spectrum_table()
    vmem = pl.BlockSpec(memory_space=pltpu.VMEM)
    smem = pl.BlockSpec(memory_space=pltpu.SMEM)
    f32, bf16 = jnp.float32, jnp.bfloat16
    return pl.pallas_call(
        functools.partial(exchange_kernel, rows, cols),
        out_shape=jax.ShapeDtypeStruct((LAGS, block, channels // cols), f32),
        in_specs=[vmem, smem, smem, vmem, vmem, vmem],
        out_specs=vmem,
        scratch_shapes=[
            pltpu.VMEM((SPAN_SEGS * own_count, WIDE), bf16),
            pltpu.VMEM((SPAN_SEGS * own_count, LANES), f32),
            pltpu.VMEM((segment_total * own_count, LANES), f32),
            pltpu.VMEM((5, FREQS * own_count, LANES), f32),
            pltpu.VMEM((count, group, 5 * LANES), bf16),
            pltpu.VMEM((count, group, 5 * LANES), bf16),
            pltpu.VMEM((group, LANES), jnp.int32),
            pltpu.VMEM((count, group, LANES), jnp.int32),
            pltpu.VMEM((count, 2 * bins * block, LANES), bf16),
            pltpu.VMEM((count, 2 * bins * block, LANES), bf16),
            pltpu.VMEM((2 * FREQS * block, LANES), f32),
            pltpu.VMEM((LAGS * block, LANES), f32),
        ]
        + [pltpu.SemaphoreType.DMA((count,))] * 6
        + [pltpu.SemaphoreType.DMA((2,))],
        compiler_params=pltpu.CompilerParams(
            collective_id=0, has_side_effects=True, vmem_limit_bytes=40 * 1024 * 1024
        ),
    )(traces, slot_channel, usable_blocks, jnp.asarray(table), jnp.asarray(taper),
      jnp.asarray(lag_table(segment_total)))


def plan(rows, cols, freqs, traces, slot_channel, usable_blocks):
    count = rows * cols
    fits = (
        freqs == 1
        and FREQS % count == 0
        and traces.shape[0] == 8
        and rows * traces.shape[0] == LANES
        and FREQS // count * traces.shape[0] % 16 == 0
        and traces.shape[1] == (2 * LANES + HALF) * SEG
    )
    if fits:
        return exchange_body(rows, cols, traces, slot_channel, usable_blocks)
    return gather_body(traces, slot_channel, usable_blocks)


def solution(mesh):
    body = functools.partial(plan, *(mesh.shape[a] for a in ("row", "col", "freq")))
    in_specs = (
        P(("groups", "row", "col"), None),
        P(("groups", "row", "col")),
        P(("groups", "row", "col")),
    )
    out_specs = P(None, ("groups", "row"), ("col", "freq"))
    return jax.shard_map(body, mesh=mesh, in_specs=in_specs, out_specs=out_specs, check_vma=False)
```

```python
import functools
import math

import jax
import jax.numpy as jnp
import numpy as np
from jax import lax
from jax.experimental import pallas as pl
from jax.experimental.pallas import tpu as pltpu
from jax.sharding import PartitionSpec as P

SEG = 300
FREQS = 64
MAXLAG = 32


water_level = 0.5
corr_gain = 3.0


def lag_weights(bin_numbers, segment_total):
    lag_steps = jnp.arange(2 * MAXLAG + 1, dtype=jnp.int32) - MAXLAG
    lag_turns = lag_steps[:, None] * bin_numbers[None, :] % SEG
    lag_angles = 2.0 * math.pi / SEG * lag_turns.astype(jnp.float32)
    norm_gain = corr_gain / math.sqrt(segment_total * FREQS)
    return jnp.stack(
        [norm_gain * jnp.cos(lag_angles), -norm_gain * jnp.sin(lag_angles)], axis=-1
    ).astype(jnp.bfloat16)

def gather_body(traces, slot_channel, usable_blocks):
    own_count = traces.shape[0]
    segment_total = traces.shape[1] // SEG
    local_bins = FREQS // lax.axis_size("freq")
    freq_index = lax.axis_index("freq")
    row_index = lax.axis_index("row")
    col_index = lax.axis_index("col")
    samples = jnp.arange(SEG, dtype=jnp.int32)
    taper = 0.5 - 0.5 * jnp.cos(2.0 * math.pi / SEG * samples.astype(jnp.float32))
    bin_numbers = 1 + freq_index * local_bins + jnp.arange(local_bins, dtype=jnp.int32)
    turns = samples[:, None] * bin_numbers[None, :] % SEG
    angles = 2.0 * math.pi / SEG * turns.astype(jnp.float32)
    dft_table = jnp.concatenate(
        [taper[:, None] * jnp.cos(angles), -taper[:, None] * jnp.sin(angles)], axis=1
    ).astype(jnp.bfloat16)
    pieces = traces.reshape(own_count, segment_total, SEG)
    coefficients = jnp.einsum("csn,nq->csq", pieces, dft_table, preferred_element_type=jnp.float32)
    windowed = pieces.astype(jnp.float32) * taper
    level = jnp.sqrt(SEG * (jnp.mean(windowed * windowed, axis=-1) + 1e-05))
    real_part = coefficients[..., :local_bins]
    imag_part = coefficients[..., local_bins:]
    divisor = (
        jnp.sqrt(real_part * real_part + imag_part * imag_part) + water_level * level[..., None]
    )
    white_real = jnp.transpose((real_part / divisor).astype(jnp.bfloat16), (0, 2, 1))
    white_imag = jnp.transpose((imag_part / divisor).astype(jnp.bfloat16), (0, 2, 1))
    own_spectra = jnp.concatenate([white_real, white_imag], axis=-1)
    block_spectra, block_slots, block_usable = (
        lax.all_gather(own_spectra, "col", axis=0, tiled=True),
        lax.all_gather(slot_channel, "col", axis=0, tiled=True),
        lax.all_gather(usable_blocks, "col", axis=0, tiled=True),
    )
    block_size = block_spectra.shape[0]
    positions = block_slots % block_size
    one_hot = (positions[None, :] == jnp.arange(block_size, dtype=jnp.int32)[:, None]).astype(
        jnp.bfloat16
    )
    ordered = jnp.einsum(
        "us,sfk->ufk", one_hot, block_spectra, preferred_element_type=jnp.float32
    ).astype(jnp.bfloat16)
    usable = jnp.repeat(block_usable, own_count, total_repeat_length=block_size).astype(
        jnp.bfloat16
    )
    ordered = ordered * usable[:, None, None]
    rotated = jnp.concatenate(
        [ordered[..., segment_total:], -ordered[..., :segment_total]], axis=-1
    )
    stacked_rows = jnp.concatenate([ordered, rotated], axis=0)
    quarter = lax.dynamic_slice_in_dim(ordered, col_index * own_count, own_count, 0)
    column_total = own_count * lax.axis_size("row")
    empty_sum = jnp.zeros((local_bins, 2 * block_size, column_total), jnp.float32)
    product = jnp.einsum(
        "afk,bfk->fab",
        stacked_rows,
        lax.all_gather(quarter, "row", axis=0, tiled=True),
        preferred_element_type=jnp.float32,
    )
    cross = lax.dynamic_update_slice_in_dim(empty_sum, product, jnp.int32(0), 2)
    stacked = cross.astype(jnp.bfloat16).reshape(local_bins, 2, block_size, column_total)
    lag_table = lag_weights(bin_numbers, segment_total)
    partial_lags = jnp.einsum(
        "lfp,fpab->lab", lag_table, stacked, preferred_element_type=jnp.float32
    )
    result = lax.psum_scatter(partial_lags, "freq", scatter_dimension=2, tiled=True)
    out_width = result.shape[2]
    columns = freq_index * out_width + jnp.arange(out_width, dtype=jnp.int32)
    column_block = columns // own_count
    column_place = col_index * own_count + columns % own_count
    row_place = jnp.arange(block_size, dtype=jnp.int32)
    same = (column_block[None, :] == row_index) & (row_place[:, None] == column_place[None, :])
    return jnp.where(same[None, :, :], jnp.float32(0.0), result)


LANES = 128
SPAN = SEG * LANES // math.gcd(SEG, LANES)
SPAN_SEGS = SPAN // SEG
WIDE = -(-SEG // LANES) * LANES
HALF = LANES // 2
LAGS = 2 * MAXLAG + 1
LAG_ROWS = -(-LAGS // 16) * 16


def spectrum_table():
    taper = 0.5 - 0.5 * np.cos(2.0 * np.pi / SEG * np.arange(SEG))
    angles = 2.0 * np.pi / SEG * (np.arange(SEG)[:, None] * np.arange(1, FREQS + 1)[None, :] % SEG)
    table = np.zeros((WIDE, 2 * FREQS), np.float32)
    table[:SEG] = taper[:, None] * np.concatenate([np.cos(angles), -np.sin(angles)], axis=1)
    wide_taper = np.zeros((8, WIDE), np.float32)
    wide_taper[:, :SEG] = taper
    return table.astype(jnp.bfloat16), wide_taper


def lag_table(segment_total, bins):
    turns = (np.arange(LAGS) - MAXLAG)[:, None] * np.arange(1, FREQS + 1)[None, :] % SEG
    angles = 2.0 * np.pi / SEG * turns
    gain = corr_gain / math.sqrt(segment_total * FREQS)
    table = np.zeros((LAG_ROWS, FREQS, 2), np.float32)
    table[:LAGS, :, 0] = gain * np.cos(angles)
    table[:LAGS, :, 1] = -gain * np.sin(angles)
    table = table.reshape(LAG_ROWS, FREQS // bins, bins, 2).transpose(0, 2, 1, 3)
    return table.reshape(LAG_ROWS, 2 * FREQS).astype(jnp.bfloat16)


PARTS = ((0, 4, (0, 3)), (4, 8, (1, 4)), (8, 10, (2,)))


def exchange_kernel(
    rows, cols, traces_in, slots, usable, table_in, taper_in, lags_in, out,
    traces, table, taper, lags, samples, powers, white, spectra,
    send_a, send_b, send_c, recv_a, recv_b, recv_c, meta, recv_meta, picks, totals,
    send2, recv2, wide2, lagged, s1, r1, sm, rm, s2, r2, own,
):
    f32, bf16 = jnp.float32, jnp.bfloat16
    count = rows * cols
    bins = FREQS // count
    own_count = traces.shape[0]
    block = own_count * cols
    channels = own_count * count
    group = bins * own_count
    width = channels // cols
    row_index, col_index = lax.axis_index("row"), lax.axis_index("col")
    me = row_index * cols + col_index
    sends, recvs = (send_a, send_b, send_c), (recv_a, recv_b, recv_c)

    fetches = []
    for number, (low, high, _) in enumerate(PARTS):
        span = pl.ds(low * SPAN, (high - low) * SPAN)
        fetches.append(
            pltpu.make_async_copy(traces_in.at[:, span], traces.at[:, span], own.at[number])
        )
    for number, (source, place) in enumerate(((table_in, table), (taper_in, taper), (lags_in, lags))):
        fetches.append(pltpu.make_async_copy(source, place, own.at[3 + number]))
    for number in (4, 0, 3, 1, 2, 5):
        fetches[number].start()

    def peer(step):
        other = lax.rem(me + step, count)
        return other, {"row": other // cols, "col": lax.rem(other, cols)}

    barrier = pltpu.get_barrier_semaphore()

    def greet(step, carry):
        pl.semaphore_signal(
            barrier, inc=1, device_id=peer(step)[1], device_id_type=pl.DeviceIdType.MESH
        )
        return carry

    lax.fori_loop(1, count, greet, 0)

    def remote(src, dst, send_sem, recv_sem, target):
        return pltpu.make_async_remote_copy(
            src_ref=src, dst_ref=dst, send_sem=send_sem, recv_sem=recv_sem,
            device_id=target, device_id_type=pl.DeviceIdType.MESH,
        )

    lane = lax.broadcasted_iota(jnp.int32, (1, LANES), 1)
    row = jnp.where(lane == own_count, usable[0], 0)
    for u in range(own_count):
        row = jnp.where(lane == u, slots[u], row)
    meta[...] = row

    def one_span(span, carry):
        for s in range(0, SPAN_SEGS, 2):
            pair = []
            for q in (s, s + 1):
                base = q * SEG // LANES * LANES
                shift = q * SEG - base
                reach = -(-(shift + SEG) // LANES) * LANES
                x = traces[:, pl.ds(pl.multiple_of(span * SPAN + base, LANES), reach)].astype(f32)
                if shift:
                    x = pltpu.roll(x, reach - shift, 1)
                x = x[:, :WIDE]
                windowed = x * taper[...]
                square = windowed * windowed
                power = square[:, :LANES]
                for t in range(1, WIDE // LANES):
                    power = power + square[:, t * LANES : (t + 1) * LANES]
                powers[q * own_count : (q + 1) * own_count, :] = power
                pair.append(x)
            samples[s * own_count : (s + 2) * own_count, :] = jnp.concatenate(pair, 0).astype(bf16)
        y = jnp.dot(samples[...], table[...], preferred_element_type=f32)
        ones = jnp.ones((LANES, LANES), bf16)
        power = powers[...]
        high = power.astype(bf16)
        rest = (power - high.astype(f32)).astype(bf16)
        power = jnp.dot(high, ones, preferred_element_type=f32) + jnp.dot(
            rest, ones, preferred_element_type=f32
        )
        level = water_level * jnp.sqrt(power + SEG * 1e-05)
        square = y * y
        magnitude = jnp.sqrt(square + pltpu.roll(square, FREQS, 1))
        depth = SPAN_SEGS * own_count
        white[pl.ds(pl.multiple_of(span * depth, depth), depth), :] = y / (magnitude + level)
        return carry

    fetches[4].wait()
    fetches[3].wait()
    for number, (low, high, tiles) in enumerate(PARTS):
        fetches[number].wait()
        lax.fori_loop(low, high, one_span, 0)
        send, recv = sends[number], recvs[number]
        for u in range(own_count):
            strip = pl.ds(u, FREQS, stride=own_count)
            depth = (high - low) * SPAN_SEGS
            z = white[pl.ds(low * SPAN_SEGS * own_count + u, depth, stride=own_count), :]
            if len(tiles) == 1:
                z = jnp.concatenate([z, pltpu.roll(z, FREQS, 1)], 0)
            z = z.T
            for half in range(len(tiles)):
                spectra[half, strip, :] = z[half * FREQS : (half + 1) * FREQS]
        for half in range(len(tiles)):
            send[:, :, half * LANES : (half + 1) * LANES] = (
                spectra[half].astype(bf16).reshape(count, group, LANES)
            )
        if number == 0:
            pl.semaphore_wait(barrier, count - 1)

            def start_meta(step, carry):
                other, target = peer(step)
                remote(meta, recv_meta.at[me], sm.at[other], rm.at[me], target).start()
                return carry

            lax.fori_loop(1, count, start_meta, 0)
            recv_meta[me] = meta[...]

        def start_part(step, carry):
            other, target = peer(step)
            remote(
                send.at[other], recv.at[me], s1.at[number, other], r1.at[number, me], target
            ).start()
            return carry

        lax.fori_loop(1, count, start_part, 0)
        recv[me] = send[me]

    def wait_meta(step, carry):
        other, target = peer(step)
        remote(meta, recv_meta.at[other], sm.at[other], rm.at[other], target).wait()
        return carry

    lax.fori_loop(1, count, wait_meta, 0)
    total = count * group
    known = recv_meta[...].reshape(count, LANES).astype(f32).astype(bf16)
    expand = (
        lax.broadcasted_iota(jnp.int32, (LANES, total), 0)
        == lax.broadcasted_iota(jnp.int32, (LANES, total), 1) % own_count
    )
    spread = jnp.dot(known, jnp.where(expand, 1.0, 0.0).astype(bf16), preferred_element_type=f32)
    source = lax.broadcasted_iota(jnp.int32, (count, total), 1) // group
    mine = source == lax.broadcasted_iota(jnp.int32, (count, total), 0)
    target_row = jnp.sum(jnp.where(mine, spread, 0.0), axis=0, keepdims=True)
    holder = lax.broadcasted_iota(jnp.int32, (channels, count), 0) // own_count
    holder = holder == lax.broadcasted_iota(jnp.int32, (channels, count), 1)
    good = jnp.dot(jnp.where(holder, 1.0, 0.0).astype(bf16), known, preferred_element_type=f32)
    good = good[:, own_count : own_count + 1]
    row_number = lax.broadcasted_iota(jnp.int32, (channels, 1), 0).astype(f32)
    bin_number = lax.broadcasted_iota(jnp.int32, (1, total), 1) // own_count % bins
    for b in range(bins):
        found = (row_number == target_row) & (bin_number == b)
        picks[b] = jnp.where(found, good, 0.0).astype(bf16)

    def start_second(b):
        def body(step, carry):
            other, target = peer(step)
            remote(
                send2.at[b, other], recv2.at[b, me], s2.at[b, other], r2.at[b, me], target
            ).start()
            return carry

        lax.fori_loop(1, count, body, 0)
        recv2[b, me] = send2[b, me]

    for number, (low, high, tiles) in enumerate(PARTS):
        send, recv = sends[number], recvs[number]

        def wait_part(step, carry):
            other, target = peer(step)
            remote(
                send.at[other], recv.at[other], s1.at[number, other], r1.at[number, other], target
            ).wait()
            return carry

        lax.fori_loop(1, count, wait_part, 0)
        depth = len(tiles) * LANES
        gathered = recv[...].reshape(total, depth)
        for b in range(bins):
            ordered = jnp.dot(picks[b], gathered, preferred_element_type=f32)
            turned = pltpu.roll(ordered, depth // 2, 1)
            sign = lax.broadcasted_iota(jnp.int32, (1, depth), 1) < depth // 2
            rotated = turned * jnp.where(sign, 1.0, -1.0)
            by_column = jnp.swapaxes(ordered.reshape(rows, cols, own_count, depth), 0, 1)
            by_column = by_column.reshape(channels, depth).astype(bf16)
            for p, left in enumerate((ordered, rotated)):
                cross = lax.dot_general(
                    left.astype(bf16), by_column, (((1,), (1,)), ((), ())),
                    preferred_element_type=f32,
                )
                if number > 0:
                    cross = cross + totals[2 * b + p]
                if number < len(PARTS) - 1:
                    totals[2 * b + p] = cross
                    continue
                cross = cross.astype(bf16)
                for r in range(rows):
                    for c in range(cols):
                        send2[b, r * cols + c, p * block : (p + 1) * block, :] = cross[
                            r * block : (r + 1) * block, c * width : (c + 1) * width
                        ]
            if number == len(PARTS) - 1:
                start_second(b)

    for b in range(bins):

        def wait_second(step, carry):
            other, target = peer(step)
            remote(
                send2.at[b, other], recv2.at[b, other], s2.at[b, other], r2.at[b, other], target
            ).wait()
            return carry

        lax.fori_loop(1, count, wait_second, 0)
        depth = count * 2 * block
        wide2[b * depth : (b + 1) * depth, :] = recv2[b].astype(f32).reshape(depth, LANES)
    fetches[5].wait()
    column = lax.broadcasted_iota(jnp.int32, (1, LANES), 1)
    for a in range(block):
        piece = wide2[pl.ds(a, 2 * FREQS, stride=block), :].astype(bf16)
        answer = jnp.dot(lags[...], piece, preferred_element_type=f32)[:LAGS]
        same = (column // own_count == row_index) & (
            col_index * own_count + column % own_count == a
        )
        lagged[pl.ds(a, LAGS, stride=block), :] = jnp.where(same, 0.0, answer)
    out[...] = lagged[...].reshape(out.shape)


def exchange_body(rows, cols, traces, slot_channel, usable_blocks):
    own_count = traces.shape[0]
    segment_total = traces.shape[1] // SEG
    count = rows * cols
    bins = FREQS // count
    block = own_count * cols
    channels = own_count * count
    group = bins * own_count
    table, taper = spectrum_table()
    lags = lag_table(segment_total, bins)
    vmem = pl.BlockSpec(memory_space=pltpu.VMEM)
    smem = pl.BlockSpec(memory_space=pltpu.SMEM)
    anywhere = pl.BlockSpec(memory_space=pl.ANY)
    f32, bf16 = jnp.float32, jnp.bfloat16
    part_shapes = [(count, group, len(tiles) * LANES) for _, _, tiles in PARTS]
    return pl.pallas_call(
        functools.partial(exchange_kernel, rows, cols),
        out_shape=jax.ShapeDtypeStruct((LAGS, block, channels // cols), f32),
        in_specs=[anywhere, smem, smem, anywhere, anywhere, anywhere],
        out_specs=vmem,
        scratch_shapes=[
            pltpu.VMEM(traces.shape, bf16),
            pltpu.VMEM(table.shape, bf16),
            pltpu.VMEM(taper.shape, f32),
            pltpu.VMEM(lags.shape, bf16),
            pltpu.VMEM((SPAN_SEGS * own_count, WIDE), bf16),
            pltpu.VMEM((SPAN_SEGS * own_count, LANES), f32),
            pltpu.VMEM((segment_total * own_count, LANES), f32),
            pltpu.VMEM((2, FREQS * own_count, LANES), f32),
        ]
        + [pltpu.VMEM(shape, bf16) for shape in part_shapes + part_shapes]
        + [
            pltpu.VMEM((1, LANES), jnp.int32),
            pltpu.VMEM((count, 1, LANES), jnp.int32),
            pltpu.VMEM((bins, channels, count * group), bf16),
            pltpu.VMEM((2 * bins, channels, channels), f32),
            pltpu.VMEM((bins, count, 2 * block, LANES), bf16),
            pltpu.VMEM((bins, count, 2 * block, LANES), bf16),
            pltpu.VMEM((2 * FREQS * block, LANES), f32),
            pltpu.VMEM((LAGS * block, LANES), f32),
            pltpu.SemaphoreType.DMA((len(PARTS), count)),
            pltpu.SemaphoreType.DMA((len(PARTS), count)),
            pltpu.SemaphoreType.DMA((count,)),
            pltpu.SemaphoreType.DMA((count,)),
            pltpu.SemaphoreType.DMA((bins, count)),
            pltpu.SemaphoreType.DMA((bins, count)),
            pltpu.SemaphoreType.DMA((6,)),
        ],
        compiler_params=pltpu.CompilerParams(
            collective_id=0, has_side_effects=True, vmem_limit_bytes=40 * 1024 * 1024
        ),
    )(traces, slot_channel, usable_blocks, jnp.asarray(table), jnp.asarray(taper),
      jnp.asarray(lags))


def plan(rows, cols, freqs, traces, slot_channel, usable_blocks):
    count = rows * cols
    fits = (
        freqs == 1
        and FREQS % count == 0
        and traces.shape[0] == 8
        and rows * traces.shape[0] == LANES
        and FREQS // count * traces.shape[0] % 16 == 0
        and traces.shape[1] == (2 * LANES + HALF) * SEG
    )
    if fits:
        return exchange_body(rows, cols, traces, slot_channel, usable_blocks)
    return gather_body(traces, slot_channel, usable_blocks)


def solution(mesh):
    body = functools.partial(plan, *(mesh.shape[a] for a in ("row", "col", "freq")))
    in_specs = (
        P(("groups", "row", "col"), None),
        P(("groups", "row", "col")),
        P(("groups", "row", "col")),
    )
    out_specs = P(None, ("groups", "row"), ("col", "freq"))
    return jax.shard_map(body, mesh=mesh, in_specs=in_specs, out_specs=out_specs, check_vma=False)
```

```python
import functools
import math

import jax
import jax.numpy as jnp
import numpy as np
from jax import lax
from jax.experimental import pallas as pl
from jax.experimental.pallas import tpu as pltpu
from jax.sharding import PartitionSpec as P

SEG = 300
FREQS = 64
MAXLAG = 32


water_level = 0.5
corr_gain = 3.0


def lag_weights(bin_numbers, segment_total):
    lag_steps = jnp.arange(2 * MAXLAG + 1, dtype=jnp.int32) - MAXLAG
    lag_turns = lag_steps[:, None] * bin_numbers[None, :] % SEG
    lag_angles = 2.0 * math.pi / SEG * lag_turns.astype(jnp.float32)
    norm_gain = corr_gain / math.sqrt(segment_total * FREQS)
    return jnp.stack(
        [norm_gain * jnp.cos(lag_angles), -norm_gain * jnp.sin(lag_angles)], axis=-1
    ).astype(jnp.bfloat16)

def gather_body(traces, slot_channel, usable_blocks):
    own_count = traces.shape[0]
    segment_total = traces.shape[1] // SEG
    local_bins = FREQS // lax.axis_size("freq")
    freq_index = lax.axis_index("freq")
    row_index = lax.axis_index("row")
    col_index = lax.axis_index("col")
    samples = jnp.arange(SEG, dtype=jnp.int32)
    taper = 0.5 - 0.5 * jnp.cos(2.0 * math.pi / SEG * samples.astype(jnp.float32))
    bin_numbers = 1 + freq_index * local_bins + jnp.arange(local_bins, dtype=jnp.int32)
    turns = samples[:, None] * bin_numbers[None, :] % SEG
    angles = 2.0 * math.pi / SEG * turns.astype(jnp.float32)
    dft_table = jnp.concatenate(
        [taper[:, None] * jnp.cos(angles), -taper[:, None] * jnp.sin(angles)], axis=1
    ).astype(jnp.bfloat16)
    pieces = traces.reshape(own_count, segment_total, SEG)
    coefficients = jnp.einsum("csn,nq->csq", pieces, dft_table, preferred_element_type=jnp.float32)
    windowed = pieces.astype(jnp.float32) * taper
    level = jnp.sqrt(SEG * (jnp.mean(windowed * windowed, axis=-1) + 1e-05))
    real_part = coefficients[..., :local_bins]
    imag_part = coefficients[..., local_bins:]
    divisor = (
        jnp.sqrt(real_part * real_part + imag_part * imag_part) + water_level * level[..., None]
    )
    white_real = jnp.transpose((real_part / divisor).astype(jnp.bfloat16), (0, 2, 1))
    white_imag = jnp.transpose((imag_part / divisor).astype(jnp.bfloat16), (0, 2, 1))
    own_spectra = jnp.concatenate([white_real, white_imag], axis=-1)
    block_spectra, block_slots, block_usable = (
        lax.all_gather(own_spectra, "col", axis=0, tiled=True),
        lax.all_gather(slot_channel, "col", axis=0, tiled=True),
        lax.all_gather(usable_blocks, "col", axis=0, tiled=True),
    )
    block_size = block_spectra.shape[0]
    positions = block_slots % block_size
    one_hot = (positions[None, :] == jnp.arange(block_size, dtype=jnp.int32)[:, None]).astype(
        jnp.bfloat16
    )
    ordered = jnp.einsum(
        "us,sfk->ufk", one_hot, block_spectra, preferred_element_type=jnp.float32
    ).astype(jnp.bfloat16)
    usable = jnp.repeat(block_usable, own_count, total_repeat_length=block_size).astype(
        jnp.bfloat16
    )
    ordered = ordered * usable[:, None, None]
    rotated = jnp.concatenate(
        [ordered[..., segment_total:], -ordered[..., :segment_total]], axis=-1
    )
    stacked_rows = jnp.concatenate([ordered, rotated], axis=0)
    quarter = lax.dynamic_slice_in_dim(ordered, col_index * own_count, own_count, 0)
    column_total = own_count * lax.axis_size("row")
    empty_sum = jnp.zeros((local_bins, 2 * block_size, column_total), jnp.float32)
    product = jnp.einsum(
        "afk,bfk->fab",
        stacked_rows,
        lax.all_gather(quarter, "row", axis=0, tiled=True),
        preferred_element_type=jnp.float32,
    )
    cross = lax.dynamic_update_slice_in_dim(empty_sum, product, jnp.int32(0), 2)
    stacked = cross.astype(jnp.bfloat16).reshape(local_bins, 2, block_size, column_total)
    lag_table = lag_weights(bin_numbers, segment_total)
    partial_lags = jnp.einsum(
        "lfp,fpab->lab", lag_table, stacked, preferred_element_type=jnp.float32
    )
    result = lax.psum_scatter(partial_lags, "freq", scatter_dimension=2, tiled=True)
    out_width = result.shape[2]
    columns = freq_index * out_width + jnp.arange(out_width, dtype=jnp.int32)
    column_block = columns // own_count
    column_place = col_index * own_count + columns % own_count
    row_place = jnp.arange(block_size, dtype=jnp.int32)
    same = (column_block[None, :] == row_index) & (row_place[:, None] == column_place[None, :])
    return jnp.where(same[None, :, :], jnp.float32(0.0), result)


LANES = 128
SPAN = SEG * LANES // math.gcd(SEG, LANES)
SPAN_SEGS = SPAN // SEG
WIDE = -(-SEG // LANES) * LANES
HALF = LANES // 2
LAGS = 2 * MAXLAG + 1
LAG_ROWS = -(-LAGS // 16) * 16


def spectrum_table():
    taper = 0.5 - 0.5 * np.cos(2.0 * np.pi / SEG * np.arange(SEG))
    angles = 2.0 * np.pi / SEG * (np.arange(SEG)[:, None] * np.arange(1, FREQS + 1)[None, :] % SEG)
    table = np.zeros((WIDE, 2 * FREQS), np.float32)
    table[:SEG] = taper[:, None] * np.concatenate([np.cos(angles), -np.sin(angles)], axis=1)
    wide_taper = np.zeros((8, WIDE), np.float32)
    wide_taper[:, :SEG] = taper
    return table.astype(jnp.bfloat16), wide_taper


def lag_table(segment_total, bins):
    turns = (np.arange(LAGS) - MAXLAG)[:, None] * np.arange(1, FREQS + 1)[None, :] % SEG
    angles = 2.0 * np.pi / SEG * turns
    gain = corr_gain / math.sqrt(segment_total * FREQS)
    table = np.zeros((LAG_ROWS, FREQS, 2), np.float32)
    table[:LAGS, :, 0] = gain * np.cos(angles)
    table[:LAGS, :, 1] = -gain * np.sin(angles)
    table = table.reshape(LAG_ROWS, FREQS // bins, bins, 2).transpose(0, 2, 1, 3)
    return table.reshape(LAG_ROWS, 2 * FREQS).astype(jnp.bfloat16)


PARTS = ((0, 4, (0, 3)), (4, 8, (1, 4)), (8, 10, (2,)))


def exchange_kernel(
    rows, cols, traces_in, slots, usable, table_in, taper_in, lags_in, out,
    traces, table, taper, lags, samples, powers, white, spectra,
    send_a, send_b, send_c, recv_a, recv_b, recv_c, meta, recv_meta, picks, totals,
    send2, recv2, wide2, lagged, s1, r1, sm, rm, s2, r2, own,
):
    f32, bf16 = jnp.float32, jnp.bfloat16
    count = rows * cols
    bins = FREQS // count
    own_count = traces.shape[0]
    block = own_count * cols
    channels = own_count * count
    group = bins * own_count
    width = channels // cols
    row_index, col_index = lax.axis_index("row"), lax.axis_index("col")
    me = row_index * cols + col_index
    sends, recvs = (send_a, send_b, send_c), (recv_a, recv_b, recv_c)

    fetches = []
    for number, (low, high, _) in enumerate(PARTS):
        span = pl.ds(low * SPAN, (high - low) * SPAN)
        fetches.append(
            pltpu.make_async_copy(traces_in.at[:, span], traces.at[:, span], own.at[number])
        )
    for number, (source, place) in enumerate(((table_in, table), (taper_in, taper), (lags_in, lags))):
        fetches.append(pltpu.make_async_copy(source, place, own.at[3 + number]))
    for number in (4, 0, 3, 1, 2, 5):
        fetches[number].start()

    def peer(step):
        other = lax.rem(me + step, count)
        return other, {"row": other // cols, "col": lax.rem(other, cols)}

    barrier = pltpu.get_barrier_semaphore()

    def greet(step, carry):
        pl.semaphore_signal(
            barrier, inc=1, device_id=peer(step)[1], device_id_type=pl.DeviceIdType.MESH
        )
        return carry

    lax.fori_loop(1, count, greet, 0)

    def remote(src, dst, send_sem, recv_sem, target):
        return pltpu.make_async_remote_copy(
            src_ref=src, dst_ref=dst, send_sem=send_sem, recv_sem=recv_sem,
            device_id=target, device_id_type=pl.DeviceIdType.MESH,
        )

    lane = lax.broadcasted_iota(jnp.int32, (1, LANES), 1)
    row = jnp.where(lane == own_count, usable[0], 0)
    for u in range(own_count):
        row = jnp.where(lane == u, slots[u], row)
    meta[...] = row

    def one_span(span, carry):
        for s in range(0, SPAN_SEGS, 2):
            pair = []
            for q in (s, s + 1):
                base = q * SEG // LANES * LANES
                shift = q * SEG - base
                reach = -(-(shift + SEG) // LANES) * LANES
                x = traces[:, pl.ds(pl.multiple_of(span * SPAN + base, LANES), reach)].astype(f32)
                if shift:
                    x = pltpu.roll(x, reach - shift, 1)
                x = x[:, :WIDE]
                windowed = x * taper[...]
                square = windowed * windowed
                power = square[:, :LANES]
                for t in range(1, WIDE // LANES):
                    power = power + square[:, t * LANES : (t + 1) * LANES]
                powers[q * own_count : (q + 1) * own_count, :] = power
                pair.append(x)
            samples[s * own_count : (s + 2) * own_count, :] = jnp.concatenate(pair, 0).astype(bf16)
        y = jnp.dot(samples[...], table[...], preferred_element_type=f32)
        ones = jnp.ones((LANES, LANES), bf16)
        power = powers[...]
        high = power.astype(bf16)
        rest = (power - high.astype(f32)).astype(bf16)
        power = jnp.dot(high, ones, preferred_element_type=f32) + jnp.dot(
            rest, ones, preferred_element_type=f32
        )
        level = water_level * jnp.sqrt(power + SEG * 1e-05)
        square = y * y
        magnitude = jnp.sqrt(square + pltpu.roll(square, FREQS, 1))
        depth = SPAN_SEGS * own_count
        white[pl.ds(pl.multiple_of(span * depth, depth), depth), :] = y / (magnitude + level)
        return carry

    fetches[4].wait()
    fetches[3].wait()
    for number, (low, high, tiles) in enumerate(PARTS):
        fetches[number].wait()
        lax.fori_loop(low, high, one_span, 0)
        send, recv = sends[number], recvs[number]
        for u in range(own_count):
            strip = pl.ds(u, FREQS, stride=own_count)
            depth = (high - low) * SPAN_SEGS
            z = white[pl.ds(low * SPAN_SEGS * own_count + u, depth, stride=own_count), :]
            if len(tiles) == 1:
                z = jnp.concatenate([z, pltpu.roll(z, FREQS, 1)], 0)
            z = z.T
            for half in range(len(tiles)):
                spectra[half, strip, :] = z[half * FREQS : (half + 1) * FREQS]
        for half in range(len(tiles)):
            send[:, :, half * LANES : (half + 1) * LANES] = (
                spectra[half].astype(bf16).reshape(count, group, LANES)
            )
        if number == 0:
            pl.semaphore_wait(barrier, count - 1)

            def start_meta(step, carry):
                other, target = peer(step)
                remote(meta, recv_meta.at[me], sm.at[other], rm.at[me], target).start()
                return carry

            lax.fori_loop(1, count, start_meta, 0)
            recv_meta[me] = meta[...]

        def start_part(step, carry):
            other, target = peer(step)
            remote(
                send.at[other], recv.at[me], s1.at[number, other], r1.at[number, me], target
            ).start()
            return carry

        lax.fori_loop(1, count, start_part, 0)
        recv[me] = send[me]

    def wait_meta(step, carry):
        other, target = peer(step)
        remote(meta, recv_meta.at[other], sm.at[other], rm.at[other], target).wait()
        return carry

    lax.fori_loop(1, count, wait_meta, 0)
    total = count * group
    known = recv_meta[...].reshape(count, LANES).astype(f32).astype(bf16)
    expand = (
        lax.broadcasted_iota(jnp.int32, (LANES, total), 0)
        == lax.broadcasted_iota(jnp.int32, (LANES, total), 1) % own_count
    )
    spread = jnp.dot(known, jnp.where(expand, 1.0, 0.0).astype(bf16), preferred_element_type=f32)
    source = lax.broadcasted_iota(jnp.int32, (count, total), 1) // group
    mine = source == lax.broadcasted_iota(jnp.int32, (count, total), 0)
    target_row = jnp.sum(jnp.where(mine, spread, 0.0), axis=0, keepdims=True)
    holder = lax.broadcasted_iota(jnp.int32, (channels, count), 0) // own_count
    holder = holder == lax.broadcasted_iota(jnp.int32, (channels, count), 1)
    good = jnp.dot(jnp.where(holder, 1.0, 0.0).astype(bf16), known, preferred_element_type=f32)
    good = good[:, own_count : own_count + 1]
    row_number = lax.broadcasted_iota(jnp.int32, (channels, 1), 0).astype(f32)
    bin_number = lax.broadcasted_iota(jnp.int32, (1, total), 1) // own_count % bins
    for b in range(bins):
        found = (row_number == target_row) & (bin_number == b)
        picks[b] = jnp.where(found, good, 0.0).astype(bf16)

    def start_second(b):
        def body(step, carry):
            other, target = peer(step)
            remote(
                send2.at[b, other], recv2.at[b, me], s2.at[b, other], r2.at[b, me], target
            ).start()
            return carry

        lax.fori_loop(1, count, body, 0)
        recv2[b, me] = send2[b, me]

    for number, (low, high, tiles) in enumerate(PARTS):
        send, recv = sends[number], recvs[number]

        def wait_part(step, carry):
            other, target = peer(step)
            remote(
                send.at[other], recv.at[other], s1.at[number, other], r1.at[number, other], target
            ).wait()
            return carry

        lax.fori_loop(1, count, wait_part, 0)
        depth = len(tiles) * LANES
        gathered = recv[...].reshape(total, depth)
        for b in range(bins):
            ordered = jnp.dot(picks[b], gathered, preferred_element_type=f32)
            turned = pltpu.roll(ordered, depth // 2, 1)
            sign = lax.broadcasted_iota(jnp.int32, (1, depth), 1) < depth // 2
            rotated = turned * jnp.where(sign, 1.0, -1.0)
            by_column = jnp.swapaxes(ordered.reshape(rows, cols, own_count, depth), 0, 1)
            by_column = by_column.reshape(channels, depth).astype(bf16)
            for p, left in enumerate((ordered, rotated)):
                cross = lax.dot_general(
                    left.astype(bf16), by_column, (((1,), (1,)), ((), ())),
                    preferred_element_type=f32,
                )
                if number > 0:
                    cross = cross + totals[2 * b + p]
                if number < len(PARTS) - 1:
                    totals[2 * b + p] = cross
                    continue
                cross = cross.astype(bf16)
                for r in range(rows):
                    for c in range(cols):
                        send2[b, r * cols + c, p * block : (p + 1) * block, :] = cross[
                            r * block : (r + 1) * block, c * width : (c + 1) * width
                        ]
            if number == len(PARTS) - 1:
                start_second(b)

    for b in range(bins):

        def wait_second(step, carry):
            other, target = peer(step)
            remote(
                send2.at[b, other], recv2.at[b, other], s2.at[b, other], r2.at[b, other], target
            ).wait()
            return carry

        lax.fori_loop(1, count, wait_second, 0)
        depth = count * 2 * block
        wide2[b * depth : (b + 1) * depth, :] = recv2[b].astype(f32).reshape(depth, LANES)
    fetches[5].wait()
    column = lax.broadcasted_iota(jnp.int32, (1, LANES), 1)
    for a in range(block):
        piece = wide2[pl.ds(a, 2 * FREQS, stride=block), :].astype(bf16)
        answer = jnp.dot(lags[...], piece, preferred_element_type=f32)[:LAGS]
        same = (column // own_count == row_index) & (
            col_index * own_count + column % own_count == a
        )
        lagged[pl.ds(a, LAGS, stride=block), :] = jnp.where(same, 0.0, answer)
    out[...] = lagged[...].reshape(out.shape)


def exchange_body(rows, cols, traces, slot_channel, usable_blocks):
    own_count = traces.shape[0]
    segment_total = traces.shape[1] // SEG
    count = rows * cols
    bins = FREQS // count
    block = own_count * cols
    channels = own_count * count
    group = bins * own_count
    table, taper = spectrum_table()
    lags = lag_table(segment_total, bins)
    vmem = pl.BlockSpec(memory_space=pltpu.VMEM)
    smem = pl.BlockSpec(memory_space=pltpu.SMEM)
    anywhere = pl.BlockSpec(memory_space=pltpu.HBM)
    f32, bf16 = jnp.float32, jnp.bfloat16
    part_shapes = [(count, group, len(tiles) * LANES) for _, _, tiles in PARTS]
    return pl.pallas_call(
        functools.partial(exchange_kernel, rows, cols),
        out_shape=jax.ShapeDtypeStruct((LAGS, block, channels // cols), f32),
        in_specs=[anywhere, smem, smem, anywhere, anywhere, anywhere],
        out_specs=vmem,
        scratch_shapes=[
            pltpu.VMEM(traces.shape, bf16),
            pltpu.VMEM(table.shape, bf16),
            pltpu.VMEM(taper.shape, f32),
            pltpu.VMEM(lags.shape, bf16),
            pltpu.VMEM((SPAN_SEGS * own_count, WIDE), bf16),
            pltpu.VMEM((SPAN_SEGS * own_count, LANES), f32),
            pltpu.VMEM((segment_total * own_count, LANES), f32),
            pltpu.VMEM((2, FREQS * own_count, LANES), f32),
        ]
        + [pltpu.VMEM(shape, bf16) for shape in part_shapes + part_shapes]
        + [
            pltpu.VMEM((1, LANES), jnp.int32),
            pltpu.VMEM((count, 1, LANES), jnp.int32),
            pltpu.VMEM((bins, channels, count * group), bf16),
            pltpu.VMEM((2 * bins, channels, channels), f32),
            pltpu.VMEM((bins, count, 2 * block, LANES), bf16),
            pltpu.VMEM((bins, count, 2 * block, LANES), bf16),
            pltpu.VMEM((2 * FREQS * block, LANES), f32),
            pltpu.VMEM((LAGS * block, LANES), f32),
            pltpu.SemaphoreType.DMA((len(PARTS), count)),
            pltpu.SemaphoreType.DMA((len(PARTS), count)),
            pltpu.SemaphoreType.DMA((count,)),
            pltpu.SemaphoreType.DMA((count,)),
            pltpu.SemaphoreType.DMA((bins, count)),
            pltpu.SemaphoreType.DMA((bins, count)),
            pltpu.SemaphoreType.DMA((6,)),
        ],
        compiler_params=pltpu.CompilerParams(
            collective_id=0, has_side_effects=True, vmem_limit_bytes=60 * 1024 * 1024
        ),
    )(traces, slot_channel, usable_blocks, jnp.asarray(table), jnp.asarray(taper),
      jnp.asarray(lags))


def plan(rows, cols, freqs, traces, slot_channel, usable_blocks):
    count = rows * cols
    fits = (
        freqs == 1
        and FREQS % count == 0
        and traces.shape[0] == 8
        and rows * traces.shape[0] == LANES
        and FREQS // count * traces.shape[0] % 16 == 0
        and traces.shape[1] == (2 * LANES + HALF) * SEG
    )
    if fits:
        return exchange_body(rows, cols, traces, slot_channel, usable_blocks)
    return gather_body(traces, slot_channel, usable_blocks)


def solution(mesh):
    body = functools.partial(plan, *(mesh.shape[a] for a in ("row", "col", "freq")))
    in_specs = (
        P(("groups", "row", "col"), None),
        P(("groups", "row", "col")),
        P(("groups", "row", "col")),
    )
    out_specs = P(None, ("groups", "row"), ("col", "freq"))
    return jax.shard_map(body, mesh=mesh, in_specs=in_specs, out_specs=out_specs, check_vma=False)
```

```python
import functools
import math

import jax
import jax.numpy as jnp
import numpy as np
from jax import lax
from jax.experimental import pallas as pl
from jax.experimental.pallas import tpu as pltpu
from jax.sharding import PartitionSpec as P

SEG = 300
FREQS = 64
MAXLAG = 32


water_level = 0.5
corr_gain = 3.0


def lag_weights(bin_numbers, segment_total):
    lag_steps = jnp.arange(2 * MAXLAG + 1, dtype=jnp.int32) - MAXLAG
    lag_turns = lag_steps[:, None] * bin_numbers[None, :] % SEG
    lag_angles = 2.0 * math.pi / SEG * lag_turns.astype(jnp.float32)
    norm_gain = corr_gain / math.sqrt(segment_total * FREQS)
    return jnp.stack(
        [norm_gain * jnp.cos(lag_angles), -norm_gain * jnp.sin(lag_angles)], axis=-1
    ).astype(jnp.bfloat16)

def gather_body(traces, slot_channel, usable_blocks):
    own_count = traces.shape[0]
    segment_total = traces.shape[1] // SEG
    local_bins = FREQS // lax.axis_size("freq")
    freq_index = lax.axis_index("freq")
    row_index = lax.axis_index("row")
    col_index = lax.axis_index("col")
    samples = jnp.arange(SEG, dtype=jnp.int32)
    taper = 0.5 - 0.5 * jnp.cos(2.0 * math.pi / SEG * samples.astype(jnp.float32))
    bin_numbers = 1 + freq_index * local_bins + jnp.arange(local_bins, dtype=jnp.int32)
    turns = samples[:, None] * bin_numbers[None, :] % SEG
    angles = 2.0 * math.pi / SEG * turns.astype(jnp.float32)
    dft_table = jnp.concatenate(
        [taper[:, None] * jnp.cos(angles), -taper[:, None] * jnp.sin(angles)], axis=1
    ).astype(jnp.bfloat16)
    pieces = traces.reshape(own_count, segment_total, SEG)
    coefficients = jnp.einsum("csn,nq->csq", pieces, dft_table, preferred_element_type=jnp.float32)
    windowed = pieces.astype(jnp.float32) * taper
    level = jnp.sqrt(SEG * (jnp.mean(windowed * windowed, axis=-1) + 1e-05))
    real_part = coefficients[..., :local_bins]
    imag_part = coefficients[..., local_bins:]
    divisor = (
        jnp.sqrt(real_part * real_part + imag_part * imag_part) + water_level * level[..., None]
    )
    white_real = jnp.transpose((real_part / divisor).astype(jnp.bfloat16), (0, 2, 1))
    white_imag = jnp.transpose((imag_part / divisor).astype(jnp.bfloat16), (0, 2, 1))
    own_spectra = jnp.concatenate([white_real, white_imag], axis=-1)
    block_spectra, block_slots, block_usable = (
        lax.all_gather(own_spectra, "col", axis=0, tiled=True),
        lax.all_gather(slot_channel, "col", axis=0, tiled=True),
        lax.all_gather(usable_blocks, "col", axis=0, tiled=True),
    )
    block_size = block_spectra.shape[0]
    positions = block_slots % block_size
    one_hot = (positions[None, :] == jnp.arange(block_size, dtype=jnp.int32)[:, None]).astype(
        jnp.bfloat16
    )
    ordered = jnp.einsum(
        "us,sfk->ufk", one_hot, block_spectra, preferred_element_type=jnp.float32
    ).astype(jnp.bfloat16)
    usable = jnp.repeat(block_usable, own_count, total_repeat_length=block_size).astype(
        jnp.bfloat16
    )
    ordered = ordered * usable[:, None, None]
    rotated = jnp.concatenate(
        [ordered[..., segment_total:], -ordered[..., :segment_total]], axis=-1
    )
    stacked_rows = jnp.concatenate([ordered, rotated], axis=0)
    quarter = lax.dynamic_slice_in_dim(ordered, col_index * own_count, own_count, 0)
    column_total = own_count * lax.axis_size("row")
    empty_sum = jnp.zeros((local_bins, 2 * block_size, column_total), jnp.float32)
    product = jnp.einsum(
        "afk,bfk->fab",
        stacked_rows,
        lax.all_gather(quarter, "row", axis=0, tiled=True),
        preferred_element_type=jnp.float32,
    )
    cross = lax.dynamic_update_slice_in_dim(empty_sum, product, jnp.int32(0), 2)
    stacked = cross.astype(jnp.bfloat16).reshape(local_bins, 2, block_size, column_total)
    lag_table = lag_weights(bin_numbers, segment_total)
    partial_lags = jnp.einsum(
        "lfp,fpab->lab", lag_table, stacked, preferred_element_type=jnp.float32
    )
    result = lax.psum_scatter(partial_lags, "freq", scatter_dimension=2, tiled=True)
    out_width = result.shape[2]
    columns = freq_index * out_width + jnp.arange(out_width, dtype=jnp.int32)
    column_block = columns // own_count
    column_place = col_index * own_count + columns % own_count
    row_place = jnp.arange(block_size, dtype=jnp.int32)
    same = (column_block[None, :] == row_index) & (row_place[:, None] == column_place[None, :])
    return jnp.where(same[None, :, :], jnp.float32(0.0), result)


LANES = 128
SPAN = SEG * LANES // math.gcd(SEG, LANES)
SPAN_SEGS = SPAN // SEG
WIDE = -(-SEG // LANES) * LANES
HALF = LANES // 2
LAGS = 2 * MAXLAG + 1
LAG_ROWS = -(-LAGS // 16) * 16


def spectrum_table():
    taper = 0.5 - 0.5 * np.cos(2.0 * np.pi / SEG * np.arange(SEG))
    angles = 2.0 * np.pi / SEG * (np.arange(SEG)[:, None] * np.arange(1, FREQS + 1)[None, :] % SEG)
    table = np.zeros((WIDE, 2 * FREQS), np.float32)
    table[:SEG] = taper[:, None] * np.concatenate([np.cos(angles), -np.sin(angles)], axis=1)
    wide_taper = np.zeros((8, WIDE), np.float32)
    wide_taper[:, :SEG] = taper
    return table.astype(jnp.bfloat16), wide_taper


def lag_table(segment_total, bins):
    turns = (np.arange(LAGS) - MAXLAG)[:, None] * np.arange(1, FREQS + 1)[None, :] % SEG
    angles = 2.0 * np.pi / SEG * turns
    gain = corr_gain / math.sqrt(segment_total * FREQS)
    table = np.zeros((LAG_ROWS, FREQS, 2), np.float32)
    table[:LAGS, :, 0] = gain * np.cos(angles)
    table[:LAGS, :, 1] = -gain * np.sin(angles)
    table = table.reshape(LAG_ROWS, -1, 2, bins, 2)
    own = table.transpose(3, 0, 1, 2, 4).reshape(bins * LAG_ROWS, -1)
    far = table.transpose(3, 0, 2, 1, 4).reshape(bins * LAG_ROWS, -1)
    return np.stack([own, far]).astype(jnp.bfloat16)


PARTS = ((0, 4, (0, 3)), (4, 8, (1, 4)), (8, 10, (2,)))


def exchange_kernel(
    rows, cols, traces_in, slots, usable, table_in, taper_in, lags_in, out,
    traces, table, taper, lags, samples, powers, white, spectra,
    send_a, send_b, send_c, near_a, near_b, near_c, far_a, far_b, far_c, meta, recv_meta,
    near_picks, far_picks, near_left, near_right, near_sum, out_sum, in_sum,
    near_send, far_send, near_recv, far_recv, near_wide, far_wide, lagged,
    s1n, r1n, s1f, r1f, sm, rm, s2n, r2n, s2f, r2f, own,
):
    f32, bf16 = jnp.float32, jnp.bfloat16
    count = rows * cols
    bins = FREQS // count
    own_count = traces.shape[0]
    block = own_count * cols
    channels = own_count * count
    group = bins * own_count
    members = count // 2
    span_channels = channels // 2
    row_index, col_index = lax.axis_index("row"), lax.axis_index("col")
    me = row_index * cols + col_index
    side, member = me // members, lax.rem(me, members)
    sends = (send_a, send_b, send_c)
    nears, fars = (near_a, near_b, near_c), (far_a, far_b, far_c)

    fetches = []
    for number, (low, high, _) in enumerate(PARTS):
        span = pl.ds(low * SPAN, (high - low) * SPAN)
        fetches.append(
            pltpu.make_async_copy(traces_in.at[:, span], traces.at[:, span], own.at[number])
        )
    for number, (source, place) in enumerate(((table_in, table), (taper_in, taper), (lags_in, lags))):
        fetches.append(pltpu.make_async_copy(source, place, own.at[3 + number]))
    for number in (4, 0, 3, 1, 2, 5):
        fetches[number].start()

    def peer(step):
        other = lax.rem(me + step, count)
        return other, {"row": other // cols, "col": lax.rem(other, cols)}

    def in_half(half, step):
        place = lax.rem(member + step, members)
        other = half * members + place
        return place, {"row": other // cols, "col": lax.rem(other, cols)}

    barrier = pltpu.get_barrier_semaphore()

    def greet(step, carry):
        pl.semaphore_signal(
            barrier, inc=1, device_id=peer(step)[1], device_id_type=pl.DeviceIdType.MESH
        )
        return carry

    lax.fori_loop(1, count, greet, 0)

    def remote(src, dst, send_sem, recv_sem, target):
        return pltpu.make_async_remote_copy(
            src_ref=src, dst_ref=dst, send_sem=send_sem, recv_sem=recv_sem,
            device_id=target, device_id_type=pl.DeviceIdType.MESH,
        )

    lane = lax.broadcasted_iota(jnp.int32, (1, LANES), 1)
    row = jnp.where(lane == own_count, usable[0], 0)
    for u in range(own_count):
        row = jnp.where(lane == u, slots[u], row)
    meta[...] = row

    def one_span(span, carry):
        for s in range(0, SPAN_SEGS, 2):
            pair = []
            for q in (s, s + 1):
                base = q * SEG // LANES * LANES
                shift = q * SEG - base
                reach = -(-(shift + SEG) // LANES) * LANES
                x = traces[:, pl.ds(pl.multiple_of(span * SPAN + base, LANES), reach)].astype(f32)
                if shift:
                    x = pltpu.roll(x, reach - shift, 1)
                x = x[:, :WIDE]
                windowed = x * taper[...]
                square = windowed * windowed
                power = square[:, :LANES]
                for t in range(1, WIDE // LANES):
                    power = power + square[:, t * LANES : (t + 1) * LANES]
                powers[q * own_count : (q + 1) * own_count, :] = power
                pair.append(x)
            samples[s * own_count : (s + 2) * own_count, :] = jnp.concatenate(pair, 0).astype(bf16)
        y = jnp.dot(samples[...], table[...], preferred_element_type=f32)
        ones = jnp.ones((LANES, LANES), bf16)
        power = powers[...]
        high = power.astype(bf16)
        rest = (power - high.astype(f32)).astype(bf16)
        power = jnp.dot(high, ones, preferred_element_type=f32) + jnp.dot(
            rest, ones, preferred_element_type=f32
        )
        level = water_level * jnp.sqrt(power + SEG * 1e-05)
        square = y * y
        magnitude = jnp.sqrt(square + pltpu.roll(square, FREQS, 1))
        depth = SPAN_SEGS * own_count
        white[pl.ds(pl.multiple_of(span * depth, depth), depth), :] = y / (magnitude + level)
        return carry

    fetches[4].wait()
    fetches[3].wait()
    for number, (low, high, tiles) in enumerate(PARTS):
        fetches[number].wait()
        lax.fori_loop(low, high, one_span, 0)
        send, near, far = sends[number], nears[number], fars[number]
        for u in range(own_count):
            strip = pl.ds(u, FREQS, stride=own_count)
            depth = (high - low) * SPAN_SEGS
            z = white[pl.ds(low * SPAN_SEGS * own_count + u, depth, stride=own_count), :]
            if len(tiles) == 1:
                z = jnp.concatenate([z, pltpu.roll(z, FREQS, 1)], 0)
            z = z.T
            for half in range(len(tiles)):
                spectra[half, strip, :] = z[half * FREQS : (half + 1) * FREQS]
        for half in range(len(tiles)):
            send[:, :, half * LANES : (half + 1) * LANES] = (
                spectra[half].astype(bf16).reshape(count, group, LANES)
            )
        if number == 0:
            pl.semaphore_wait(barrier, count - 1)

            def start_meta(step, carry):
                other, target = peer(step)
                remote(meta, recv_meta.at[me], sm.at[other], rm.at[me], target).start()
                return carry

            lax.fori_loop(1, count, start_meta, 0)
            recv_meta[me] = meta[...]

        def start_far(step):
            place, target = in_half(1 - side, step)
            remote(
                send.at[2 * place + 1 - side], far.at[member],
                s1f.at[number, place], r1f.at[number, member], target,
            ).start()

        def start_part(step, carry):
            start_far(step)
            place, target = in_half(side, step)
            remote(
                send.at[pl.ds(2 * place, 2)], near.at[member],
                s1n.at[number, place], r1n.at[number, member], target,
            ).start()
            return carry

        start_far(0)
        lax.fori_loop(1, members, start_part, 0)
        near[member] = send[pl.ds(2 * member, 2)]

    def wait_meta(step, carry):
        other, target = peer(step)
        remote(meta, recv_meta.at[other], sm.at[other], rm.at[other], target).wait()
        return carry

    lax.fori_loop(1, count, wait_meta, 0)
    known = recv_meta[...].reshape(count, LANES).astype(f32).astype(bf16)

    def choose(half, pieces, picks):
        each = pieces * group
        total = members * each
        expand = (
            lax.broadcasted_iota(jnp.int32, (LANES, total), 0)
            == lax.broadcasted_iota(jnp.int32, (LANES, total), 1) % own_count
        )
        expand = jnp.where(expand, 1.0, 0.0).astype(bf16)
        spread = jnp.dot(known, expand, preferred_element_type=f32)
        source = lax.broadcasted_iota(jnp.int32, (count, total), 1) // each + half * members
        mine = source == lax.broadcasted_iota(jnp.int32, (count, total), 0)
        target_row = jnp.sum(jnp.where(mine, spread, 0.0), axis=0, keepdims=True)
        holder = lax.broadcasted_iota(jnp.int32, (span_channels, count), 0) // own_count
        holder = holder + half * members
        holder = holder == lax.broadcasted_iota(jnp.int32, (span_channels, count), 1)
        good = jnp.dot(jnp.where(holder, 1.0, 0.0).astype(bf16), known, preferred_element_type=f32)
        good = good[:, own_count : own_count + 1]
        row_number = lax.broadcasted_iota(jnp.int32, (span_channels, 1), 0) + half * span_channels
        row_number = row_number.astype(f32)
        bin_number = lax.broadcasted_iota(jnp.int32, (1, total), 1) // own_count % (pieces * bins)
        for b in range(pieces * bins):
            found = (row_number == target_row) & (bin_number == b)
            picks[b] = jnp.where(found, good, 0.0).astype(bf16)

    choose(side, 2, near_picks)
    choose(1 - side, 1, far_picks)

    def sides(pick, gathered):
        depth = gathered.shape[1]
        ordered = jnp.dot(pick, gathered, preferred_element_type=f32)
        turned = pltpu.roll(ordered, depth // 2, 1)
        sign = lax.broadcasted_iota(jnp.int32, (1, depth), 1) < depth // 2
        rotated = turned * jnp.where(sign, 1.0, -1.0)
        by_column = jnp.swapaxes(ordered.reshape(rows // 2, cols, own_count, depth), 0, 1)
        left = jnp.concatenate([ordered.astype(bf16), rotated.astype(bf16)], 0)
        return left, by_column.reshape(span_channels, depth).astype(bf16)

    def pairs(left, right):
        return lax.dot_general(
            left, right, (((1,), (1,)), ((), ())), preferred_element_type=f32
        )

    first_lanes = lane < HALF

    def place_units(even, odd, store):
        units = (
            jnp.where(first_lanes, even, pltpu.roll(odd, HALF, 1)).astype(bf16),
            jnp.where(first_lanes, pltpu.roll(even, HALF, 1), odd).astype(bf16),
        )
        for c in range(cols):
            for r in range(rows // 2):
                for p in range(2):
                    low = p * span_channels + r * block
                    store(r * cols + c, p * block, units[c][low : low + block, :])

    def store_far(place, low, unit):
        far_send[place, low : low + block, :] = unit

    def store_near(number):
        def store(place, low, unit):
            near_send[place, number, low : low + block, :] = unit

        return store

    for number, (_, _, tiles) in enumerate(PARTS):
        send, near, far = sends[number], nears[number], fars[number]

        def wait_far(step):
            place, target = in_half(1 - side, step)
            remote(
                send.at[2 * place + 1 - side], far.at[place],
                s1f.at[number, place], r1f.at[number, place], target,
            ).wait()

        def wait_part(step, carry):
            wait_far(step)
            place, target = in_half(side, step)
            remote(
                send.at[pl.ds(2 * place, 2)], near.at[place],
                s1n.at[number, place], r1n.at[number, place], target,
            ).wait()
            return carry

        wait_far(0)
        lax.fori_loop(1, members, wait_part, 0)
        depth = len(tiles) * LANES
        near_rows = near[...].reshape(members * 2 * group, depth)
        far_rows = far[...].reshape(members * group, depth)
        for q in range(2 * bins):
            left, right = sides(near_picks[q], near_rows)
            near_left[q, :, :depth] = left
            near_right[q, :, :depth] = right
        last = number == len(PARTS) - 1
        for b in range(bins):
            left, right = sides(far_picks[b], far_rows)
            inward = pairs(left, near_right[side * bins + b, :, :depth])
            outward = pairs(near_left[side * bins + b, :, :depth], right)
            if number > 0:
                inward = inward + in_sum[b]
                outward = outward + out_sum[b]
            in_sum[b] = inward
            out_sum[b] = outward
        if last:
            place_units(in_sum[0], in_sum[1], store_far)

            def start_far_second(step, carry):
                place, target = in_half(1 - side, step)
                remote(
                    far_send.at[place], far_recv.at[member], s2f.at[place], r2f.at[member], target
                ).start()
                return carry

            lax.fori_loop(0, members, start_far_second, 0)
        for q in range(2 * bins):
            cross = pairs(near_left[q, :, :depth], near_right[q, :, :depth])
            near_sum[q] = cross + near_sum[q] if number > 0 else cross
    place_units(near_sum[0], near_sum[1], store_near(0))
    place_units(near_sum[2], near_sum[3], store_near(1))
    place_units(out_sum[0], out_sum[1], store_near(2))

    def start_near_second(step, carry):
        place, target = in_half(side, step)
        remote(
            near_send.at[place], near_recv.at[member], s2n.at[place], r2n.at[member], target
        ).start()
        return carry

    lax.fori_loop(1, members, start_near_second, 0)
    near_recv[member] = near_send[member]

    def wait_far_second(step, carry):
        place, target = in_half(1 - side, step)
        remote(
            far_send.at[place], far_recv.at[place], s2f.at[place], r2f.at[place], target
        ).wait()
        return carry

    def wait_near_second(step, carry):
        place, target = in_half(side, step)
        remote(
            near_send.at[place], near_recv.at[place], s2n.at[place], r2n.at[place], target
        ).wait()
        return carry

    lax.fori_loop(0, members, wait_far_second, 0)
    depth = members * 2 * block
    far_wide[pl.ds(pl.multiple_of((1 - side) * depth, depth), depth), :] = (
        far_recv[...].astype(f32).reshape(depth, LANES)
    )
    lax.fori_loop(1, members, wait_near_second, 0)
    far_wide[pl.ds(pl.multiple_of(side * depth, depth), depth), :] = (
        near_recv[:, 2].astype(f32).reshape(depth, LANES)
    )
    near_wide[...] = near_recv[:, :2].astype(f32).reshape(2 * depth, LANES)
    fetches[5].wait()
    column = lax.broadcasted_iota(jnp.int32, (1, LANES), 1)
    for a in range(block):
        answers = []
        for number, wide in enumerate((near_wide, far_wide)):
            piece = wide[pl.ds(a, FREQS, stride=block), :].astype(bf16)
            both = jnp.dot(lags[number], piece, preferred_element_type=f32)
            answers.append(both[:LAG_ROWS] + pltpu.roll(both[LAG_ROWS:], HALF, 1))
        left = jnp.where(side == 0, answers[0], answers[1])
        right = jnp.where(side == 0, answers[1], answers[0])
        answer = jnp.where(first_lanes, left, pltpu.roll(right, HALF, 1))[:LAGS]
        same = (column // own_count == row_index) & (
            col_index * own_count + column % own_count == a
        )
        lagged[pl.ds(a, LAGS, stride=block), :] = jnp.where(same, 0.0, answer)
    out[...] = lagged[...].reshape(out.shape)


def exchange_body(rows, cols, traces, slot_channel, usable_blocks):
    own_count = traces.shape[0]
    segment_total = traces.shape[1] // SEG
    count = rows * cols
    bins = FREQS // count
    block = own_count * cols
    channels = own_count * count
    group = bins * own_count
    table, taper = spectrum_table()
    lags = lag_table(segment_total, bins)
    vmem = pl.BlockSpec(memory_space=pltpu.VMEM)
    smem = pl.BlockSpec(memory_space=pltpu.SMEM)
    anywhere = pl.BlockSpec(memory_space=pltpu.HBM)
    f32, bf16 = jnp.float32, jnp.bfloat16
    members, span_channels = count // 2, channels // 2
    depths = [len(tiles) * LANES for _, _, tiles in PARTS]
    part_shapes = [(count, group, depth) for depth in depths]
    part_shapes += [(members, 2, group, depth) for depth in depths]
    part_shapes += [(members, group, depth) for depth in depths]
    return pl.pallas_call(
        functools.partial(exchange_kernel, rows, cols),
        out_shape=jax.ShapeDtypeStruct((LAGS, block, channels // cols), f32),
        in_specs=[anywhere, smem, smem, anywhere, anywhere, anywhere],
        out_specs=vmem,
        scratch_shapes=[
            pltpu.VMEM(traces.shape, bf16),
            pltpu.VMEM(table.shape, bf16),
            pltpu.VMEM(taper.shape, f32),
            pltpu.VMEM(lags.shape, bf16),
            pltpu.VMEM((SPAN_SEGS * own_count, WIDE), bf16),
            pltpu.VMEM((SPAN_SEGS * own_count, LANES), f32),
            pltpu.VMEM((segment_total * own_count, LANES), f32),
            pltpu.VMEM((2, FREQS * own_count, LANES), f32),
        ]
        + [pltpu.VMEM(shape, bf16) for shape in part_shapes]
        + [
            pltpu.VMEM((1, LANES), jnp.int32),
            pltpu.VMEM((count, 1, LANES), jnp.int32),
            pltpu.VMEM((2 * bins, span_channels, members * 2 * group), bf16),
            pltpu.VMEM((bins, span_channels, members * group), bf16),
            pltpu.VMEM((2 * bins, 2 * span_channels, 2 * LANES), bf16),
            pltpu.VMEM((2 * bins, span_channels, 2 * LANES), bf16),
            pltpu.VMEM((2 * bins, 2 * span_channels, LANES), f32),
            pltpu.VMEM((bins, 2 * span_channels, LANES), f32),
            pltpu.VMEM((bins, 2 * span_channels, LANES), f32),
            pltpu.VMEM((members, 3, 2 * block, LANES), bf16),
            pltpu.VMEM((members, 2 * block, LANES), bf16),
            pltpu.VMEM((members, 3, 2 * block, LANES), bf16),
            pltpu.VMEM((members, 2 * block, LANES), bf16),
            pltpu.VMEM((FREQS * block, LANES), f32),
            pltpu.VMEM((FREQS * block, LANES), f32),
            pltpu.VMEM((LAGS * block, LANES), f32),
        ]
        + [pltpu.SemaphoreType.DMA((len(PARTS), members))] * 4
        + [pltpu.SemaphoreType.DMA((count,))] * 2
        + [pltpu.SemaphoreType.DMA((members,))] * 4
        + [
            pltpu.SemaphoreType.DMA((6,)),
        ],
        compiler_params=pltpu.CompilerParams(
            collective_id=0, has_side_effects=True, vmem_limit_bytes=60 * 1024 * 1024
        ),
    )(traces, slot_channel, usable_blocks, jnp.asarray(table), jnp.asarray(taper),
      jnp.asarray(lags))


def plan(rows, cols, freqs, traces, slot_channel, usable_blocks):
    count = rows * cols
    fits = (
        freqs == 1
        and FREQS == 2 * count
        and cols == 2
        and rows % 2 == 0
        and traces.shape[0] == 8
        and rows * traces.shape[0] == LANES
        and FREQS // count * traces.shape[0] % 16 == 0
        and traces.shape[1] == (2 * LANES + HALF) * SEG
    )
    if fits:
        return exchange_body(rows, cols, traces, slot_channel, usable_blocks)
    return gather_body(traces, slot_channel, usable_blocks)


def solution(mesh):
    body = functools.partial(plan, *(mesh.shape[a] for a in ("row", "col", "freq")))
    in_specs = (
        P(("groups", "row", "col"), None),
        P(("groups", "row", "col")),
        P(("groups", "row", "col")),
    )
    out_specs = P(None, ("groups", "row"), ("col", "freq"))
    return jax.shard_map(body, mesh=mesh, in_specs=in_specs, out_specs=out_specs, check_vma=False)
```

```python
import functools
import math

import jax
import jax.numpy as jnp
import numpy as np
from jax import lax
from jax.experimental import pallas as pl
from jax.experimental.pallas import tpu as pltpu
from jax.sharding import PartitionSpec as P

SEG = 300
FREQS = 64
MAXLAG = 32


water_level = 0.5
corr_gain = 3.0


def lag_weights(bin_numbers, segment_total):
    lag_steps = jnp.arange(2 * MAXLAG + 1, dtype=jnp.int32) - MAXLAG
    lag_turns = lag_steps[:, None] * bin_numbers[None, :] % SEG
    lag_angles = 2.0 * math.pi / SEG * lag_turns.astype(jnp.float32)
    norm_gain = corr_gain / math.sqrt(segment_total * FREQS)
    return jnp.stack(
        [norm_gain * jnp.cos(lag_angles), -norm_gain * jnp.sin(lag_angles)], axis=-1
    ).astype(jnp.bfloat16)

def gather_body(traces, slot_channel, usable_blocks):
    own_count = traces.shape[0]
    segment_total = traces.shape[1] // SEG
    local_bins = FREQS // lax.axis_size("freq")
    freq_index = lax.axis_index("freq")
    row_index = lax.axis_index("row")
    col_index = lax.axis_index("col")
    samples = jnp.arange(SEG, dtype=jnp.int32)
    taper = 0.5 - 0.5 * jnp.cos(2.0 * math.pi / SEG * samples.astype(jnp.float32))
    bin_numbers = 1 + freq_index * local_bins + jnp.arange(local_bins, dtype=jnp.int32)
    turns = samples[:, None] * bin_numbers[None, :] % SEG
    angles = 2.0 * math.pi / SEG * turns.astype(jnp.float32)
    dft_table = jnp.concatenate(
        [taper[:, None] * jnp.cos(angles), -taper[:, None] * jnp.sin(angles)], axis=1
    ).astype(jnp.bfloat16)
    pieces = traces.reshape(own_count, segment_total, SEG)
    coefficients = jnp.einsum("csn,nq->csq", pieces, dft_table, preferred_element_type=jnp.float32)
    windowed = pieces.astype(jnp.float32) * taper
    level = jnp.sqrt(SEG * (jnp.mean(windowed * windowed, axis=-1) + 1e-05))
    real_part = coefficients[..., :local_bins]
    imag_part = coefficients[..., local_bins:]
    divisor = (
        jnp.sqrt(real_part * real_part + imag_part * imag_part) + water_level * level[..., None]
    )
    white_real = jnp.transpose((real_part / divisor).astype(jnp.bfloat16), (0, 2, 1))
    white_imag = jnp.transpose((imag_part / divisor).astype(jnp.bfloat16), (0, 2, 1))
    own_spectra = jnp.concatenate([white_real, white_imag], axis=-1)
    block_spectra, block_slots, block_usable = (
        lax.all_gather(own_spectra, "col", axis=0, tiled=True),
        lax.all_gather(slot_channel, "col", axis=0, tiled=True),
        lax.all_gather(usable_blocks, "col", axis=0, tiled=True),
    )
    block_size = block_spectra.shape[0]
    positions = block_slots % block_size
    one_hot = (positions[None, :] == jnp.arange(block_size, dtype=jnp.int32)[:, None]).astype(
        jnp.bfloat16
    )
    ordered = jnp.einsum(
        "us,sfk->ufk", one_hot, block_spectra, preferred_element_type=jnp.float32
    ).astype(jnp.bfloat16)
    usable = jnp.repeat(block_usable, own_count, total_repeat_length=block_size).astype(
        jnp.bfloat16
    )
    ordered = ordered * usable[:, None, None]
    rotated = jnp.concatenate(
        [ordered[..., segment_total:], -ordered[..., :segment_total]], axis=-1
    )
    stacked_rows = jnp.concatenate([ordered, rotated], axis=0)
    quarter = lax.dynamic_slice_in_dim(ordered, col_index * own_count, own_count, 0)
    column_total = own_count * lax.axis_size("row")
    empty_sum = jnp.zeros((local_bins, 2 * block_size, column_total), jnp.float32)
    product = jnp.einsum(
        "afk,bfk->fab",
        stacked_rows,
        lax.all_gather(quarter, "row", axis=0, tiled=True),
        preferred_element_type=jnp.float32,
    )
    cross = lax.dynamic_update_slice_in_dim(empty_sum, product, jnp.int32(0), 2)
    stacked = cross.astype(jnp.bfloat16).reshape(local_bins, 2, block_size, column_total)
    lag_table = lag_weights(bin_numbers, segment_total)
    partial_lags = jnp.einsum(
        "lfp,fpab->lab", lag_table, stacked, preferred_element_type=jnp.float32
    )
    result = lax.psum_scatter(partial_lags, "freq", scatter_dimension=2, tiled=True)
    out_width = result.shape[2]
    columns = freq_index * out_width + jnp.arange(out_width, dtype=jnp.int32)
    column_block = columns // own_count
    column_place = col_index * own_count + columns % own_count
    row_place = jnp.arange(block_size, dtype=jnp.int32)
    same = (column_block[None, :] == row_index) & (row_place[:, None] == column_place[None, :])
    return jnp.where(same[None, :, :], jnp.float32(0.0), result)


LANES = 128
SPAN = SEG * LANES // math.gcd(SEG, LANES)
SPAN_SEGS = SPAN // SEG
WIDE = -(-SEG // LANES) * LANES
HALF = LANES // 2
LAGS = 2 * MAXLAG + 1
LAG_ROWS = -(-LAGS // 16) * 16


def spectrum_table():
    taper = 0.5 - 0.5 * np.cos(2.0 * np.pi / SEG * np.arange(SEG))
    angles = 2.0 * np.pi / SEG * (np.arange(SEG)[:, None] * np.arange(1, FREQS + 1)[None, :] % SEG)
    table = np.zeros((WIDE, 2 * FREQS), np.float32)
    table[:SEG] = taper[:, None] * np.concatenate([np.cos(angles), -np.sin(angles)], axis=1)
    wide_taper = np.zeros((8, WIDE), np.float32)
    wide_taper[:, :SEG] = taper
    return table.astype(jnp.bfloat16), wide_taper


def lag_table(segment_total, bins):
    turns = (np.arange(LAGS) - MAXLAG)[:, None] * np.arange(1, FREQS + 1)[None, :] % SEG
    angles = 2.0 * np.pi / SEG * turns
    gain = corr_gain / math.sqrt(segment_total * FREQS)
    table = np.zeros((LAG_ROWS, FREQS, 2), np.float32)
    table[:LAGS, :, 0] = gain * np.cos(angles)
    table[:LAGS, :, 1] = -gain * np.sin(angles)
    table = table.reshape(LAG_ROWS, -1, 2, bins, 2)
    own = table.transpose(3, 0, 1, 2, 4).reshape(bins * LAG_ROWS, -1)
    far = table.transpose(3, 0, 2, 1, 4).reshape(bins * LAG_ROWS, -1)
    return np.stack([own, far]).astype(jnp.bfloat16)


PARTS = ((0, 4, (0, 3)), (4, 8, (1, 4)), (8, 10, (2,)))


def exchange_kernel(
    rows, cols, traces_in, slots_in, usable_in, table_in, taper_in, lags_in, out,
    traces, table, taper, lags, samples, powers, white, spectra,
    send_a, send_b, send_c, near_a, near_b, near_c, far_a, far_b, far_c, meta, recv_meta,
    near_picks, far_picks, near_left, near_right, near_sum, out_sum, in_sum,
    near_send, far_send, near_recv, far_recv, near_wide, far_wide, lagged,
    s1n, r1n, s1f, r1f, sm, rm, s2n, r2n, s2f, r2f, own, slots, usable,
):
    f32, bf16 = jnp.float32, jnp.bfloat16
    count = rows * cols
    bins = FREQS // count
    own_count = traces.shape[0]
    block = own_count * cols
    channels = own_count * count
    group = bins * own_count
    members = count // 2
    span_channels = channels // 2
    row_index, col_index = lax.axis_index("row"), lax.axis_index("col")
    me = row_index * cols + col_index
    side, member = me // members, lax.rem(me, members)
    sends = (send_a, send_b, send_c)
    nears, fars = (near_a, near_b, near_c), (far_a, far_b, far_c)

    fetches = []
    for number, (low, high, _) in enumerate(PARTS):
        span = pl.ds(low * SPAN, (high - low) * SPAN)
        fetches.append(
            pltpu.make_async_copy(traces_in.at[:, span], traces.at[:, span], own.at[number])
        )
    for number, (source, place) in enumerate(((table_in, table), (taper_in, taper), (lags_in, lags))):
        fetches.append(pltpu.make_async_copy(source, place, own.at[3 + number]))
    fetches.append(pltpu.make_async_copy(slots_in, slots, own.at[6]))
    fetches.append(pltpu.make_async_copy(usable_in, usable, own.at[7]))
    for number in (4, 0, 3, 1, 2, 5, 6, 7):
        fetches[number].start()

    def peer(step):
        other = lax.rem(me + step, count)
        return other, {"row": other // cols, "col": lax.rem(other, cols)}

    def in_half(half, step):
        place = lax.rem(member + step, members)
        other = half * members + place
        return place, {"row": other // cols, "col": lax.rem(other, cols)}

    barrier = pltpu.get_barrier_semaphore()

    def greet(step, carry):
        pl.semaphore_signal(
            barrier, inc=1, device_id=peer(step)[1], device_id_type=pl.DeviceIdType.MESH
        )
        return carry

    lax.fori_loop(1, count, greet, 0)

    def remote(src, dst, send_sem, recv_sem, target):
        return pltpu.make_async_remote_copy(
            src_ref=src, dst_ref=dst, send_sem=send_sem, recv_sem=recv_sem,
            device_id=target, device_id_type=pl.DeviceIdType.MESH,
        )

    fetches[6].wait()
    fetches[7].wait()
    lane = lax.broadcasted_iota(jnp.int32, (1, LANES), 1)
    row = jnp.where(lane == own_count, usable[0], 0)
    for u in range(own_count):
        row = jnp.where(lane == u, slots[u], row)
    meta[...] = row

    def one_span(span, carry):
        for s in range(0, SPAN_SEGS, 2):
            pair = []
            for q in (s, s + 1):
                base = q * SEG // LANES * LANES
                shift = q * SEG - base
                reach = -(-(shift + SEG) // LANES) * LANES
                x = traces[:, pl.ds(pl.multiple_of(span * SPAN + base, LANES), reach)].astype(f32)
                if shift:
                    x = pltpu.roll(x, reach - shift, 1)
                x = x[:, :WIDE]
                windowed = x * taper[...]
                square = windowed * windowed
                power = square[:, :LANES]
                for t in range(1, WIDE // LANES):
                    power = power + square[:, t * LANES : (t + 1) * LANES]
                powers[q * own_count : (q + 1) * own_count, :] = power
                pair.append(x)
            samples[s * own_count : (s + 2) * own_count, :] = jnp.concatenate(pair, 0).astype(bf16)
        y = jnp.dot(samples[...], table[...], preferred_element_type=f32)
        ones = jnp.ones((LANES, LANES), bf16)
        power = powers[...]
        high = power.astype(bf16)
        rest = (power - high.astype(f32)).astype(bf16)
        power = jnp.dot(high, ones, preferred_element_type=f32) + jnp.dot(
            rest, ones, preferred_element_type=f32
        )
        level = water_level * jnp.sqrt(power + SEG * 1e-05)
        square = y * y
        magnitude = jnp.sqrt(square + pltpu.roll(square, FREQS, 1))
        depth = SPAN_SEGS * own_count
        white[pl.ds(pl.multiple_of(span * depth, depth), depth), :] = y / (magnitude + level)
        return carry

    fetches[4].wait()
    fetches[3].wait()
    for number, (low, high, tiles) in enumerate(PARTS):
        fetches[number].wait()
        lax.fori_loop(low, high, one_span, 0)
        send, near, far = sends[number], nears[number], fars[number]
        for u in range(own_count):
            strip = pl.ds(u, FREQS, stride=own_count)
            depth = (high - low) * SPAN_SEGS
            z = white[pl.ds(low * SPAN_SEGS * own_count + u, depth, stride=own_count), :]
            if len(tiles) == 1:
                z = jnp.concatenate([z, pltpu.roll(z, FREQS, 1)], 0)
            z = z.T
            for half in range(len(tiles)):
                spectra[half, strip, :] = z[half * FREQS : (half + 1) * FREQS]
        for half in range(len(tiles)):
            send[:, :, half * LANES : (half + 1) * LANES] = (
                spectra[half].astype(bf16).reshape(count, group, LANES)
            )
        if number == 0:
            pl.semaphore_wait(barrier, count - 1)

        def start_far(step):
            place, target = in_half(1 - side, step)
            remote(
                send.at[2 * place + 1 - side], far.at[member],
                s1f.at[number, place], r1f.at[number, member], target,
            ).start()

        def start_part(step, carry):
            start_far(step)
            place, target = in_half(side, step)
            remote(
                send.at[pl.ds(2 * place, 2)], near.at[member],
                s1n.at[number, place], r1n.at[number, member], target,
            ).start()
            return carry

        start_far(0)
        lax.fori_loop(1, members, start_part, 0)
        near[member] = send[pl.ds(2 * member, 2)]
        if number == 0:

            def start_meta(step, carry):
                other, target = peer(step)
                remote(meta, recv_meta.at[me], sm.at[other], rm.at[me], target).start()
                return carry

            lax.fori_loop(1, count, start_meta, 0)
            recv_meta[me] = meta[...]

    def wait_meta(step, carry):
        other, target = peer(step)
        remote(meta, recv_meta.at[other], sm.at[other], rm.at[other], target).wait()
        return carry

    lax.fori_loop(1, count, wait_meta, 0)
    known = recv_meta[...].reshape(count, LANES).astype(f32).astype(bf16)

    def choose(half, pieces, picks):
        each = pieces * group
        total = members * each
        expand = (
            lax.broadcasted_iota(jnp.int32, (LANES, total), 0)
            == lax.broadcasted_iota(jnp.int32, (LANES, total), 1) % own_count
        )
        expand = jnp.where(expand, 1.0, 0.0).astype(bf16)
        spread = jnp.dot(known, expand, preferred_element_type=f32)
        source = lax.broadcasted_iota(jnp.int32, (count, total), 1) // each + half * members
        mine = source == lax.broadcasted_iota(jnp.int32, (count, total), 0)
        target_row = jnp.sum(jnp.where(mine, spread, 0.0), axis=0, keepdims=True)
        holder = lax.broadcasted_iota(jnp.int32, (span_channels, count), 0) // own_count
        holder = holder + half * members
        holder = holder == lax.broadcasted_iota(jnp.int32, (span_channels, count), 1)
        good = jnp.dot(jnp.where(holder, 1.0, 0.0).astype(bf16), known, preferred_element_type=f32)
        good = good[:, own_count : own_count + 1]
        row_number = lax.broadcasted_iota(jnp.int32, (span_channels, 1), 0) + half * span_channels
        row_number = row_number.astype(f32)
        bin_number = lax.broadcasted_iota(jnp.int32, (1, total), 1) // own_count % (pieces * bins)
        for b in range(pieces * bins):
            found = (row_number == target_row) & (bin_number == b)
            picks[b] = jnp.where(found, good, 0.0).astype(bf16)

    choose(side, 2, near_picks)
    choose(1 - side, 1, far_picks)

    def sides(pick, gathered):
        depth = gathered.shape[1]
        ordered = jnp.dot(pick, gathered, preferred_element_type=f32)
        turned = pltpu.roll(ordered, depth // 2, 1)
        sign = lax.broadcasted_iota(jnp.int32, (1, depth), 1) < depth // 2
        rotated = turned * jnp.where(sign, 1.0, -1.0)
        by_column = jnp.swapaxes(ordered.reshape(rows // 2, cols, own_count, depth), 0, 1)
        left = jnp.concatenate([ordered.astype(bf16), rotated.astype(bf16)], 0)
        return left, by_column.reshape(span_channels, depth).astype(bf16)

    def pairs(left, right):
        return lax.dot_general(
            left, right, (((1,), (1,)), ((), ())), preferred_element_type=f32
        )

    first_lanes = lane < HALF

    def place_units(even, odd, store):
        units = (
            jnp.where(first_lanes, even, pltpu.roll(odd, HALF, 1)).astype(bf16),
            jnp.where(first_lanes, pltpu.roll(even, HALF, 1), odd).astype(bf16),
        )
        for c in range(cols):
            for r in range(rows // 2):
                for p in range(2):
                    low = p * span_channels + r * block
                    store(r * cols + c, p * block, units[c][low : low + block, :])

    def store_far(place, low, unit):
        far_send[place, low : low + block, :] = unit

    def store_near(number):
        def store(place, low, unit):
            near_send[place, number, low : low + block, :] = unit

        return store

    for number, (_, _, tiles) in enumerate(PARTS):
        send, near, far = sends[number], nears[number], fars[number]

        def wait_far(step):
            place, target = in_half(1 - side, step)
            remote(
                send.at[2 * place + 1 - side], far.at[place],
                s1f.at[number, place], r1f.at[number, place], target,
            ).wait()

        def wait_part(step, carry):
            wait_far(step)
            place, target = in_half(side, step)
            remote(
                send.at[pl.ds(2 * place, 2)], near.at[place],
                s1n.at[number, place], r1n.at[number, place], target,
            ).wait()
            return carry

        wait_far(0)
        lax.fori_loop(1, members, wait_part, 0)
        depth = len(tiles) * LANES
        near_rows = near[...].reshape(members * 2 * group, depth)
        far_rows = far[...].reshape(members * group, depth)

        def order_near(half):
            for b in range(bins):
                q = half * bins + b
                left, right = sides(near_picks[q], near_rows)
                near_left[q, :, :depth] = left
                near_right[q, :, :depth] = right

        order_near(side)
        last = number == len(PARTS) - 1
        for b in range(bins):
            left, right = sides(far_picks[b], far_rows)
            inward = pairs(left, near_right[side * bins + b, :, :depth])
            outward = pairs(near_left[side * bins + b, :, :depth], right)
            if number > 0:
                inward = inward + in_sum[b]
                outward = outward + out_sum[b]
            in_sum[b] = inward
            out_sum[b] = outward
        if last:
            place_units(in_sum[0], in_sum[1], store_far)

            def start_far_second(step, carry):
                place, target = in_half(1 - side, step)
                remote(
                    far_send.at[place], far_recv.at[member], s2f.at[place], r2f.at[member], target
                ).start()
                return carry

            lax.fori_loop(0, members, start_far_second, 0)
        order_near(1 - side)
        for q in range(2 * bins):
            cross = pairs(near_left[q, :, :depth], near_right[q, :, :depth])
            near_sum[q] = cross + near_sum[q] if number > 0 else cross
    place_units(near_sum[0], near_sum[1], store_near(0))
    place_units(near_sum[2], near_sum[3], store_near(1))
    place_units(out_sum[0], out_sum[1], store_near(2))

    def start_near_second(step, carry):
        place, target = in_half(side, step)
        remote(
            near_send.at[place], near_recv.at[member], s2n.at[place], r2n.at[member], target
        ).start()
        return carry

    lax.fori_loop(1, members, start_near_second, 0)
    near_recv[member] = near_send[member]

    def wait_far_second(step, carry):
        place, target = in_half(1 - side, step)
        remote(
            far_send.at[place], far_recv.at[place], s2f.at[place], r2f.at[place], target
        ).wait()
        return carry

    def wait_near_second(step, carry):
        place, target = in_half(side, step)
        remote(
            near_send.at[place], near_recv.at[place], s2n.at[place], r2n.at[place], target
        ).wait()
        return carry

    lax.fori_loop(0, members, wait_far_second, 0)
    depth = members * 2 * block
    far_wide[pl.ds(pl.multiple_of((1 - side) * depth, depth), depth), :] = (
        far_recv[...].astype(f32).reshape(depth, LANES)
    )
    lax.fori_loop(1, members, wait_near_second, 0)
    far_wide[pl.ds(pl.multiple_of(side * depth, depth), depth), :] = (
        near_recv[:, 2].astype(f32).reshape(depth, LANES)
    )
    near_wide[...] = near_recv[:, :2].astype(f32).reshape(2 * depth, LANES)
    fetches[5].wait()
    column = lax.broadcasted_iota(jnp.int32, (1, LANES), 1)
    for a in range(block):
        answers = []
        for number, wide in enumerate((near_wide, far_wide)):
            piece = wide[pl.ds(a, FREQS, stride=block), :].astype(bf16)
            both = jnp.dot(lags[number], piece, preferred_element_type=f32)
            answers.append(both[:LAG_ROWS] + pltpu.roll(both[LAG_ROWS:], HALF, 1))
        left = jnp.where(side == 0, answers[0], answers[1])
        right = jnp.where(side == 0, answers[1], answers[0])
        answer = jnp.where(first_lanes, left, pltpu.roll(right, HALF, 1))[:LAGS]
        same = (column // own_count == row_index) & (
            col_index * own_count + column % own_count == a
        )
        lagged[pl.ds(a, LAGS, stride=block), :] = jnp.where(same, 0.0, answer)
    out[...] = lagged[...].reshape(out.shape)


def exchange_body(rows, cols, traces, slot_channel, usable_blocks):
    own_count = traces.shape[0]
    segment_total = traces.shape[1] // SEG
    count = rows * cols
    bins = FREQS // count
    block = own_count * cols
    channels = own_count * count
    group = bins * own_count
    table, taper = spectrum_table()
    lags = lag_table(segment_total, bins)
    vmem = pl.BlockSpec(memory_space=pltpu.VMEM)
    anywhere = pl.BlockSpec(memory_space=pltpu.HBM)
    f32, bf16 = jnp.float32, jnp.bfloat16
    members, span_channels = count // 2, channels // 2
    depths = [len(tiles) * LANES for _, _, tiles in PARTS]
    part_shapes = [(count, group, depth) for depth in depths]
    part_shapes += [(members, 2, group, depth) for depth in depths]
    part_shapes += [(members, group, depth) for depth in depths]
    return pl.pallas_call(
        functools.partial(exchange_kernel, rows, cols),
        out_shape=jax.ShapeDtypeStruct((LAGS, block, channels // cols), f32),
        in_specs=[anywhere, anywhere, anywhere, anywhere, anywhere, anywhere],
        out_specs=vmem,
        scratch_shapes=[
            pltpu.VMEM(traces.shape, bf16),
            pltpu.VMEM(table.shape, bf16),
            pltpu.VMEM(taper.shape, f32),
            pltpu.VMEM(lags.shape, bf16),
            pltpu.VMEM((SPAN_SEGS * own_count, WIDE), bf16),
            pltpu.VMEM((SPAN_SEGS * own_count, LANES), f32),
            pltpu.VMEM((segment_total * own_count, LANES), f32),
            pltpu.VMEM((2, FREQS * own_count, LANES), f32),
        ]
        + [pltpu.VMEM(shape, bf16) for shape in part_shapes]
        + [
            pltpu.VMEM((1, LANES), jnp.int32),
            pltpu.VMEM((count, 1, LANES), jnp.int32),
            pltpu.VMEM((2 * bins, span_channels, members * 2 * group), bf16),
            pltpu.VMEM((bins, span_channels, members * group), bf16),
            pltpu.VMEM((2 * bins, 2 * span_channels, 2 * LANES), bf16),
            pltpu.VMEM((2 * bins, span_channels, 2 * LANES), bf16),
            pltpu.VMEM((2 * bins, 2 * span_channels, LANES), f32),
            pltpu.VMEM((bins, 2 * span_channels, LANES), f32),
            pltpu.VMEM((bins, 2 * span_channels, LANES), f32),
            pltpu.VMEM((members, 3, 2 * block, LANES), bf16),
            pltpu.VMEM((members, 2 * block, LANES), bf16),
            pltpu.VMEM((members, 3, 2 * block, LANES), bf16),
            pltpu.VMEM((members, 2 * block, LANES), bf16),
            pltpu.VMEM((FREQS * block, LANES), f32),
            pltpu.VMEM((FREQS * block, LANES), f32),
            pltpu.VMEM((LAGS * block, LANES), f32),
        ]
        + [pltpu.SemaphoreType.DMA((len(PARTS), members))] * 4
        + [pltpu.SemaphoreType.DMA((count,))] * 2
        + [pltpu.SemaphoreType.DMA((members,))] * 4
        + [
            pltpu.SemaphoreType.DMA((8,)),
            pltpu.SMEM(slot_channel.shape, jnp.int32),
            pltpu.SMEM(usable_blocks.shape, jnp.int32),
        ],
        compiler_params=pltpu.CompilerParams(
            collective_id=0, has_side_effects=True, vmem_limit_bytes=60 * 1024 * 1024
        ),
    )(traces, slot_channel, usable_blocks, jnp.asarray(table), jnp.asarray(taper),
      jnp.asarray(lags))


def plan(rows, cols, freqs, traces, slot_channel, usable_blocks):
    count = rows * cols
    fits = (
        freqs == 1
        and FREQS == 2 * count
        and cols == 2
        and rows % 2 == 0
        and traces.shape[0] == 8
        and rows * traces.shape[0] == LANES
        and FREQS // count * traces.shape[0] % 16 == 0
        and traces.shape[1] == (2 * LANES + HALF) * SEG
    )
    if fits:
        return exchange_body(rows, cols, traces, slot_channel, usable_blocks)
    return gather_body(traces, slot_channel, usable_blocks)


def solution(mesh):
    body = functools.partial(plan, *(mesh.shape[a] for a in ("row", "col", "freq")))
    in_specs = (
        P(("groups", "row", "col"), None),
        P(("groups", "row", "col")),
        P(("groups", "row", "col")),
    )
    out_specs = P(None, ("groups", "row"), ("col", "freq"))
    return jax.shard_map(body, mesh=mesh, in_specs=in_specs, out_specs=out_specs, check_vma=False)
```

```python
import functools
import math

import jax
import jax.numpy as jnp
import numpy as np
from jax import lax
from jax.experimental import pallas as pl
from jax.experimental.pallas import tpu as pltpu
from jax.sharding import PartitionSpec as P

SEG = 300
FREQS = 64
MAXLAG = 32


water_level = 0.5
corr_gain = 3.0


def lag_weights(bin_numbers, segment_total):
    lag_steps = jnp.arange(2 * MAXLAG + 1, dtype=jnp.int32) - MAXLAG
    lag_turns = lag_steps[:, None] * bin_numbers[None, :] % SEG
    lag_angles = 2.0 * math.pi / SEG * lag_turns.astype(jnp.float32)
    norm_gain = corr_gain / math.sqrt(segment_total * FREQS)
    return jnp.stack(
        [norm_gain * jnp.cos(lag_angles), -norm_gain * jnp.sin(lag_angles)], axis=-1
    ).astype(jnp.bfloat16)

def gather_body(traces, slot_channel, usable_blocks):
    own_count = traces.shape[0]
    segment_total = traces.shape[1] // SEG
    local_bins = FREQS // lax.axis_size("freq")
    freq_index = lax.axis_index("freq")
    row_index = lax.axis_index("row")
    col_index = lax.axis_index("col")
    samples = jnp.arange(SEG, dtype=jnp.int32)
    taper = 0.5 - 0.5 * jnp.cos(2.0 * math.pi / SEG * samples.astype(jnp.float32))
    bin_numbers = 1 + freq_index * local_bins + jnp.arange(local_bins, dtype=jnp.int32)
    turns = samples[:, None] * bin_numbers[None, :] % SEG
    angles = 2.0 * math.pi / SEG * turns.astype(jnp.float32)
    dft_table = jnp.concatenate(
        [taper[:, None] * jnp.cos(angles), -taper[:, None] * jnp.sin(angles)], axis=1
    ).astype(jnp.bfloat16)
    pieces = traces.reshape(own_count, segment_total, SEG)
    coefficients = jnp.einsum("csn,nq->csq", pieces, dft_table, preferred_element_type=jnp.float32)
    windowed = pieces.astype(jnp.float32) * taper
    level = jnp.sqrt(SEG * (jnp.mean(windowed * windowed, axis=-1) + 1e-05))
    real_part = coefficients[..., :local_bins]
    imag_part = coefficients[..., local_bins:]
    divisor = (
        jnp.sqrt(real_part * real_part + imag_part * imag_part) + water_level * level[..., None]
    )
    white_real = jnp.transpose((real_part / divisor).astype(jnp.bfloat16), (0, 2, 1))
    white_imag = jnp.transpose((imag_part / divisor).astype(jnp.bfloat16), (0, 2, 1))
    own_spectra = jnp.concatenate([white_real, white_imag], axis=-1)
    block_spectra, block_slots, block_usable = (
        lax.all_gather(own_spectra, "col", axis=0, tiled=True),
        lax.all_gather(slot_channel, "col", axis=0, tiled=True),
        lax.all_gather(usable_blocks, "col", axis=0, tiled=True),
    )
    block_size = block_spectra.shape[0]
    positions = block_slots % block_size
    one_hot = (positions[None, :] == jnp.arange(block_size, dtype=jnp.int32)[:, None]).astype(
        jnp.bfloat16
    )
    ordered = jnp.einsum(
        "us,sfk->ufk", one_hot, block_spectra, preferred_element_type=jnp.float32
    ).astype(jnp.bfloat16)
    usable = jnp.repeat(block_usable, own_count, total_repeat_length=block_size).astype(
        jnp.bfloat16
    )
    ordered = ordered * usable[:, None, None]
    rotated = jnp.concatenate(
        [ordered[..., segment_total:], -ordered[..., :segment_total]], axis=-1
    )
    stacked_rows = jnp.concatenate([ordered, rotated], axis=0)
    quarter = lax.dynamic_slice_in_dim(ordered, col_index * own_count, own_count, 0)
    column_total = own_count * lax.axis_size("row")
    empty_sum = jnp.zeros((local_bins, 2 * block_size, column_total), jnp.float32)
    product = jnp.einsum(
        "afk,bfk->fab",
        stacked_rows,
        lax.all_gather(quarter, "row", axis=0, tiled=True),
        preferred_element_type=jnp.float32,
    )
    cross = lax.dynamic_update_slice_in_dim(empty_sum, product, jnp.int32(0), 2)
    stacked = cross.astype(jnp.bfloat16).reshape(local_bins, 2, block_size, column_total)
    lag_table = lag_weights(bin_numbers, segment_total)
    partial_lags = jnp.einsum(
        "lfp,fpab->lab", lag_table, stacked, preferred_element_type=jnp.float32
    )
    result = lax.psum_scatter(partial_lags, "freq", scatter_dimension=2, tiled=True)
    out_width = result.shape[2]
    columns = freq_index * out_width + jnp.arange(out_width, dtype=jnp.int32)
    column_block = columns // own_count
    column_place = col_index * own_count + columns % own_count
    row_place = jnp.arange(block_size, dtype=jnp.int32)
    same = (column_block[None, :] == row_index) & (row_place[:, None] == column_place[None, :])
    return jnp.where(same[None, :, :], jnp.float32(0.0), result)


LANES = 128
SPAN = SEG * LANES // math.gcd(SEG, LANES)
SPAN_SEGS = SPAN // SEG
WIDE = -(-SEG // LANES) * LANES
HALF = LANES // 2
LAGS = 2 * MAXLAG + 1
LAG_ROWS = -(-LAGS // 16) * 16


def spectrum_table():
    taper = 0.5 - 0.5 * np.cos(2.0 * np.pi / SEG * np.arange(SEG))
    angles = 2.0 * np.pi / SEG * (np.arange(SEG)[:, None] * np.arange(1, FREQS + 1)[None, :] % SEG)
    table = np.zeros((WIDE, 2 * FREQS), np.float32)
    table[:SEG] = taper[:, None] * np.concatenate([np.cos(angles), -np.sin(angles)], axis=1)
    wide_taper = np.zeros((8, WIDE), np.float32)
    wide_taper[:, :SEG] = taper
    return table.astype(jnp.bfloat16), wide_taper


def lag_table(segment_total, bins):
    turns = (np.arange(LAGS) - MAXLAG)[:, None] * np.arange(1, FREQS + 1)[None, :] % SEG
    angles = 2.0 * np.pi / SEG * turns
    gain = corr_gain / math.sqrt(segment_total * FREQS)
    table = np.zeros((LAG_ROWS, FREQS, 2), np.float32)
    table[:LAGS, :, 0] = gain * np.cos(angles)
    table[:LAGS, :, 1] = -gain * np.sin(angles)
    table = table.reshape(LAG_ROWS, -1, 2, bins, 2)
    own = table.transpose(3, 0, 1, 2, 4).reshape(bins * LAG_ROWS, -1)
    far = table.transpose(3, 0, 2, 1, 4).reshape(bins * LAG_ROWS, -1)
    return np.stack([own, far]).astype(jnp.bfloat16)


PARTS = ((0, 4, (0, 3)), (4, 8, (1, 4)), (8, 10, (2,)))


def exchange_kernel(
    rows, cols, traces_in, slots_in, usable_in, table_in, taper_in, lags_in, out,
    traces, table, taper, lags, samples, powers, white, spectra,
    send_a, send_b, send_c, near_a, near_b, near_c, far_a, far_b, far_c, meta, recv_meta,
    near_picks, far_picks, near_left, near_right, near_sum, out_sum, in_sum,
    near_send, far_send, near_recv, far_recv, near_wide, far_wide, lagged,
    s1n, r1n, s1f, r1f, sm, rm, s2n, r2n, s2f, r2f, own, slots, usable,
):
    f32, bf16 = jnp.float32, jnp.bfloat16
    count = rows * cols
    bins = FREQS // count
    own_count = traces.shape[0]
    block = own_count * cols
    channels = own_count * count
    group = bins * own_count
    members = count // 2
    span_channels = channels // 2
    row_index, col_index = lax.axis_index("row"), lax.axis_index("col")
    me = row_index * cols + col_index
    side, member = me // members, lax.rem(me, members)
    sends = (send_a, send_b, send_c)
    nears, fars = (near_a, near_b, near_c), (far_a, far_b, far_c)

    fetches = []
    for number, (low, high, _) in enumerate(PARTS):
        span = pl.ds(low * SPAN, (high - low) * SPAN)
        fetches.append(
            pltpu.make_async_copy(traces_in.at[:, span], traces.at[:, span], own.at[number])
        )
    for number, (source, place) in enumerate(((table_in, table), (taper_in, taper), (lags_in, lags))):
        fetches.append(pltpu.make_async_copy(source, place, own.at[3 + number]))
    fetches.append(pltpu.make_async_copy(slots_in, slots, own.at[6]))
    fetches.append(pltpu.make_async_copy(usable_in, usable, own.at[7]))
    for number in (4, 0, 3, 1, 2, 5, 6, 7):
        fetches[number].start()

    def peer(step):
        other = lax.rem(me + step, count)
        return other, {"row": other // cols, "col": lax.rem(other, cols)}

    def in_half(half, step):
        place = lax.rem(member + step, members)
        other = half * members + place
        return place, {"row": other // cols, "col": lax.rem(other, cols)}

    barrier = pltpu.get_barrier_semaphore()

    def greet(step, carry):
        pl.semaphore_signal(
            barrier, inc=1, device_id=peer(step)[1], device_id_type=pl.DeviceIdType.MESH
        )
        return carry

    lax.fori_loop(1, count, greet, 0, unroll=True)

    def remote(src, dst, send_sem, recv_sem, target):
        return pltpu.make_async_remote_copy(
            src_ref=src, dst_ref=dst, send_sem=send_sem, recv_sem=recv_sem,
            device_id=target, device_id_type=pl.DeviceIdType.MESH,
        )

    fetches[6].wait()
    fetches[7].wait()
    lane = lax.broadcasted_iota(jnp.int32, (1, LANES), 1)
    row = jnp.where(lane == own_count, usable[0], 0)
    for u in range(own_count):
        row = jnp.where(lane == u, slots[u], row)
    meta[...] = row

    def one_span(span, carry):
        for s in range(0, SPAN_SEGS, 2):
            pair = []
            for q in (s, s + 1):
                base = q * SEG // LANES * LANES
                shift = q * SEG - base
                reach = -(-(shift + SEG) // LANES) * LANES
                x = traces[:, pl.ds(pl.multiple_of(span * SPAN + base, LANES), reach)].astype(f32)
                if shift:
                    x = pltpu.roll(x, reach - shift, 1)
                x = x[:, :WIDE]
                windowed = x * taper[...]
                square = windowed * windowed
                power = square[:, :LANES]
                for t in range(1, WIDE // LANES):
                    power = power + square[:, t * LANES : (t + 1) * LANES]
                powers[q * own_count : (q + 1) * own_count, :] = power
                pair.append(x)
            samples[s * own_count : (s + 2) * own_count, :] = jnp.concatenate(pair, 0).astype(bf16)
        y = jnp.dot(samples[...], table[...], preferred_element_type=f32)
        ones = jnp.ones((LANES, LANES), bf16)
        power = powers[...]
        high = power.astype(bf16)
        rest = (power - high.astype(f32)).astype(bf16)
        power = jnp.dot(high, ones, preferred_element_type=f32) + jnp.dot(
            rest, ones, preferred_element_type=f32
        )
        level = water_level * jnp.sqrt(power + SEG * 1e-05)
        square = y * y
        magnitude = jnp.sqrt(square + pltpu.roll(square, FREQS, 1))
        depth = SPAN_SEGS * own_count
        white[pl.ds(pl.multiple_of(span * depth, depth), depth), :] = y / (magnitude + level)
        return carry

    fetches[4].wait()
    fetches[3].wait()
    for number, (low, high, tiles) in enumerate(PARTS):
        fetches[number].wait()
        lax.fori_loop(low, high, one_span, 0)
        send, near, far = sends[number], nears[number], fars[number]
        for u in range(own_count):
            strip = pl.ds(u, FREQS, stride=own_count)
            depth = (high - low) * SPAN_SEGS
            z = white[pl.ds(low * SPAN_SEGS * own_count + u, depth, stride=own_count), :]
            if len(tiles) == 1:
                z = jnp.concatenate([z, pltpu.roll(z, FREQS, 1)], 0)
            z = z.T
            for half in range(len(tiles)):
                spectra[half, strip, :] = z[half * FREQS : (half + 1) * FREQS]
        for half in range(len(tiles)):
            send[:, :, half * LANES : (half + 1) * LANES] = (
                spectra[half].astype(bf16).reshape(count, group, LANES)
            )
        if number == 0:
            pl.semaphore_wait(barrier, count - 1)

        def start_far(step):
            place, target = in_half(1 - side, step)
            remote(
                send.at[2 * place + 1 - side], far.at[member],
                s1f.at[number, place], r1f.at[number, member], target,
            ).start()

        def start_part(step, carry):
            start_far(step)
            place, target = in_half(side, step)
            remote(
                send.at[pl.ds(2 * place, 2)], near.at[member],
                s1n.at[number, place], r1n.at[number, member], target,
            ).start()
            return carry

        start_far(0)
        lax.fori_loop(1, members, start_part, 0, unroll=True)
        near[member] = send[pl.ds(2 * member, 2)]
        if number == 0:

            def start_meta(step, carry):
                other, target = peer(step)
                remote(meta, recv_meta.at[me], sm.at[other], rm.at[me], target).start()
                return carry

            lax.fori_loop(1, count, start_meta, 0, unroll=True)
            recv_meta[me] = meta[...]

    def wait_meta(step, carry):
        other, target = peer(step)
        remote(meta, recv_meta.at[other], sm.at[other], rm.at[other], target).wait()
        return carry

    lax.fori_loop(1, count, wait_meta, 0, unroll=True)
    known = recv_meta[...].reshape(count, LANES).astype(f32).astype(bf16)

    def choose(half, pieces, picks):
        each = pieces * group
        total = members * each
        expand = (
            lax.broadcasted_iota(jnp.int32, (LANES, total), 0)
            == lax.broadcasted_iota(jnp.int32, (LANES, total), 1) % own_count
        )
        expand = jnp.where(expand, 1.0, 0.0).astype(bf16)
        spread = jnp.dot(known, expand, preferred_element_type=f32)
        source = lax.broadcasted_iota(jnp.int32, (count, total), 1) // each + half * members
        mine = source == lax.broadcasted_iota(jnp.int32, (count, total), 0)
        target_row = jnp.sum(jnp.where(mine, spread, 0.0), axis=0, keepdims=True)
        holder = lax.broadcasted_iota(jnp.int32, (span_channels, count), 0) // own_count
        holder = holder + half * members
        holder = holder == lax.broadcasted_iota(jnp.int32, (span_channels, count), 1)
        good = jnp.dot(jnp.where(holder, 1.0, 0.0).astype(bf16), known, preferred_element_type=f32)
        good = good[:, own_count : own_count + 1]
        row_number = lax.broadcasted_iota(jnp.int32, (span_channels, 1), 0) + half * span_channels
        row_number = row_number.astype(f32)
        bin_number = lax.broadcasted_iota(jnp.int32, (1, total), 1) // own_count % (pieces * bins)
        for b in range(pieces * bins):
            found = (row_number == target_row) & (bin_number == b)
            picks[b] = jnp.where(found, good, 0.0).astype(bf16)

    choose(side, 2, near_picks)
    choose(1 - side, 1, far_picks)

    def sides(pick, gathered):
        depth = gathered.shape[1]
        ordered = jnp.dot(pick, gathered, preferred_element_type=f32)
        turned = pltpu.roll(ordered, depth // 2, 1)
        sign = lax.broadcasted_iota(jnp.int32, (1, depth), 1) < depth // 2
        rotated = turned * jnp.where(sign, 1.0, -1.0)
        by_column = jnp.swapaxes(ordered.reshape(rows // 2, cols, own_count, depth), 0, 1)
        left = jnp.concatenate([ordered.astype(bf16), rotated.astype(bf16)], 0)
        return left, by_column.reshape(span_channels, depth).astype(bf16)

    def pairs(left, right):
        return lax.dot_general(
            left, right, (((1,), (1,)), ((), ())), preferred_element_type=f32
        )

    first_lanes = lane < HALF

    def place_units(even, odd, store):
        units = (
            jnp.where(first_lanes, even, pltpu.roll(odd, HALF, 1)).astype(bf16),
            jnp.where(first_lanes, pltpu.roll(even, HALF, 1), odd).astype(bf16),
        )
        for c in range(cols):
            for r in range(rows // 2):
                for p in range(2):
                    low = p * span_channels + r * block
                    store(r * cols + c, p * block, units[c][low : low + block, :])

    def store_far(place, low, unit):
        far_send[place, low : low + block, :] = unit

    def store_near(number):
        def store(place, low, unit):
            near_send[place, number, low : low + block, :] = unit

        return store

    for number, (_, _, tiles) in enumerate(PARTS):
        send, near, far = sends[number], nears[number], fars[number]

        def wait_far(step):
            place, target = in_half(1 - side, step)
            remote(
                send.at[2 * place + 1 - side], far.at[place],
                s1f.at[number, place], r1f.at[number, place], target,
            ).wait()

        def wait_part(step, carry):
            wait_far(step)
            place, target = in_half(side, step)
            remote(
                send.at[pl.ds(2 * place, 2)], near.at[place],
                s1n.at[number, place], r1n.at[number, place], target,
            ).wait()
            return carry

        wait_far(0)
        lax.fori_loop(1, members, wait_part, 0, unroll=True)
        depth = len(tiles) * LANES
        near_rows = near[...].reshape(members * 2 * group, depth)
        far_rows = far[...].reshape(members * group, depth)

        def order_near(half):
            for b in range(bins):
                q = half * bins + b
                left, right = sides(near_picks[q], near_rows)
                near_left[q, :, :depth] = left
                near_right[q, :, :depth] = right

        order_near(side)
        last = number == len(PARTS) - 1
        for b in range(bins):
            left, right = sides(far_picks[b], far_rows)
            inward = pairs(left, near_right[side * bins + b, :, :depth])
            outward = pairs(near_left[side * bins + b, :, :depth], right)
            if number > 0:
                inward = inward + in_sum[b]
                outward = outward + out_sum[b]
            in_sum[b] = inward
            out_sum[b] = outward
        if last:
            place_units(in_sum[0], in_sum[1], store_far)

            def start_far_second(step, carry):
                place, target = in_half(1 - side, step)
                remote(
                    far_send.at[place], far_recv.at[member], s2f.at[place], r2f.at[member], target
                ).start()
                return carry

            lax.fori_loop(0, members, start_far_second, 0, unroll=True)
        order_near(1 - side)
        for q in range(2 * bins):
            cross = pairs(near_left[q, :, :depth], near_right[q, :, :depth])
            near_sum[q] = cross + near_sum[q] if number > 0 else cross
    place_units(near_sum[0], near_sum[1], store_near(0))
    place_units(near_sum[2], near_sum[3], store_near(1))
    place_units(out_sum[0], out_sum[1], store_near(2))

    def start_near_second(step, carry):
        place, target = in_half(side, step)
        remote(
            near_send.at[place], near_recv.at[member], s2n.at[place], r2n.at[member], target
        ).start()
        return carry

    lax.fori_loop(1, members, start_near_second, 0, unroll=True)
    near_recv[member] = near_send[member]

    def wait_far_second(step, carry):
        place, target = in_half(1 - side, step)
        remote(
            far_send.at[place], far_recv.at[place], s2f.at[place], r2f.at[place], target
        ).wait()
        return carry

    def wait_near_second(step, carry):
        place, target = in_half(side, step)
        remote(
            near_send.at[place], near_recv.at[place], s2n.at[place], r2n.at[place], target
        ).wait()
        return carry

    lax.fori_loop(0, members, wait_far_second, 0, unroll=True)
    depth = members * 2 * block
    far_wide[pl.ds(pl.multiple_of((1 - side) * depth, depth), depth), :] = (
        far_recv[...].astype(f32).reshape(depth, LANES)
    )
    lax.fori_loop(1, members, wait_near_second, 0, unroll=True)
    far_wide[pl.ds(pl.multiple_of(side * depth, depth), depth), :] = (
        near_recv[:, 2].astype(f32).reshape(depth, LANES)
    )
    near_wide[...] = near_recv[:, :2].astype(f32).reshape(2 * depth, LANES)
    fetches[5].wait()
    column = lax.broadcasted_iota(jnp.int32, (1, LANES), 1)
    for a in range(block):
        answers = []
        for number, wide in enumerate((near_wide, far_wide)):
            piece = wide[pl.ds(a, FREQS, stride=block), :].astype(bf16)
            both = jnp.dot(lags[number], piece, preferred_element_type=f32)
            answers.append(both[:LAG_ROWS] + pltpu.roll(both[LAG_ROWS:], HALF, 1))
        left = jnp.where(side == 0, answers[0], answers[1])
        right = jnp.where(side == 0, answers[1], answers[0])
        answer = jnp.where(first_lanes, left, pltpu.roll(right, HALF, 1))[:LAGS]
        same = (column // own_count == row_index) & (
            col_index * own_count + column % own_count == a
        )
        lagged[pl.ds(a, LAGS, stride=block), :] = jnp.where(same, 0.0, answer)
    out[...] = lagged[...].reshape(out.shape)


def exchange_body(rows, cols, traces, slot_channel, usable_blocks):
    own_count = traces.shape[0]
    segment_total = traces.shape[1] // SEG
    count = rows * cols
    bins = FREQS // count
    block = own_count * cols
    channels = own_count * count
    group = bins * own_count
    table, taper = spectrum_table()
    lags = lag_table(segment_total, bins)
    vmem = pl.BlockSpec(memory_space=pltpu.VMEM)
    anywhere = pl.BlockSpec(memory_space=pltpu.HBM)
    f32, bf16 = jnp.float32, jnp.bfloat16
    members, span_channels = count // 2, channels // 2
    depths = [len(tiles) * LANES for _, _, tiles in PARTS]
    part_shapes = [(count, group, depth) for depth in depths]
    part_shapes += [(members, 2, group, depth) for depth in depths]
    part_shapes += [(members, group, depth) for depth in depths]
    return pl.pallas_call(
        functools.partial(exchange_kernel, rows, cols),
        out_shape=jax.ShapeDtypeStruct((LAGS, block, channels // cols), f32),
        in_specs=[anywhere, anywhere, anywhere, anywhere, anywhere, anywhere],
        out_specs=vmem,
        scratch_shapes=[
            pltpu.VMEM(traces.shape, bf16),
            pltpu.VMEM(table.shape, bf16),
            pltpu.VMEM(taper.shape, f32),
            pltpu.VMEM(lags.shape, bf16),
            pltpu.VMEM((SPAN_SEGS * own_count, WIDE), bf16),
            pltpu.VMEM((SPAN_SEGS * own_count, LANES), f32),
            pltpu.VMEM((segment_total * own_count, LANES), f32),
            pltpu.VMEM((2, FREQS * own_count, LANES), f32),
        ]
        + [pltpu.VMEM(shape, bf16) for shape in part_shapes]
        + [
            pltpu.VMEM((1, LANES), jnp.int32),
            pltpu.VMEM((count, 1, LANES), jnp.int32),
            pltpu.VMEM((2 * bins, span_channels, members * 2 * group), bf16),
            pltpu.VMEM((bins, span_channels, members * group), bf16),
            pltpu.VMEM((2 * bins, 2 * span_channels, 2 * LANES), bf16),
            pltpu.VMEM((2 * bins, span_channels, 2 * LANES), bf16),
            pltpu.VMEM((2 * bins, 2 * span_channels, LANES), f32),
            pltpu.VMEM((bins, 2 * span_channels, LANES), f32),
            pltpu.VMEM((bins, 2 * span_channels, LANES), f32),
            pltpu.VMEM((members, 3, 2 * block, LANES), bf16),
            pltpu.VMEM((members, 2 * block, LANES), bf16),
            pltpu.VMEM((members, 3, 2 * block, LANES), bf16),
            pltpu.VMEM((members, 2 * block, LANES), bf16),
            pltpu.VMEM((FREQS * block, LANES), f32),
            pltpu.VMEM((FREQS * block, LANES), f32),
            pltpu.VMEM((LAGS * block, LANES), f32),
        ]
        + [pltpu.SemaphoreType.DMA((len(PARTS), members))] * 4
        + [pltpu.SemaphoreType.DMA((count,))] * 2
        + [pltpu.SemaphoreType.DMA((members,))] * 4
        + [
            pltpu.SemaphoreType.DMA((8,)),
            pltpu.SMEM(slot_channel.shape, jnp.int32),
            pltpu.SMEM(usable_blocks.shape, jnp.int32),
        ],
        compiler_params=pltpu.CompilerParams(
            collective_id=0, has_side_effects=True, vmem_limit_bytes=60 * 1024 * 1024
        ),
    )(traces, slot_channel, usable_blocks, jnp.asarray(table), jnp.asarray(taper),
      jnp.asarray(lags))


def plan(rows, cols, freqs, traces, slot_channel, usable_blocks):
    count = rows * cols
    fits = (
        freqs == 1
        and FREQS == 2 * count
        and cols == 2
        and rows % 2 == 0
        and traces.shape[0] == 8
        and rows * traces.shape[0] == LANES
        and FREQS // count * traces.shape[0] % 16 == 0
        and traces.shape[1] == (2 * LANES + HALF) * SEG
    )
    if fits:
        return exchange_body(rows, cols, traces, slot_channel, usable_blocks)
    return gather_body(traces, slot_channel, usable_blocks)


def solution(mesh):
    body = functools.partial(plan, *(mesh.shape[a] for a in ("row", "col", "freq")))
    in_specs = (
        P(("groups", "row", "col"), None),
        P(("groups", "row", "col")),
        P(("groups", "row", "col")),
    )
    out_specs = P(None, ("groups", "row"), ("col", "freq"))
    return jax.shard_map(body, mesh=mesh, in_specs=in_specs, out_specs=out_specs, check_vma=False)
```
